32 devices in a mesh: segment: 4 (over y, x), frame: 2 (over core), row: 4 (over z).
Axes of the slice: x: 2, y: 2, z: 4, core: 2. Of those that a mesh axis runs over, the one named last changes fastest.
Arguments:
- latents: bfloat16 [2, 4, 8, 24, 320], P(None, 'frame', 'row')
- cotangent: bfloat16 [2, 4, 8, 24, 320], P(None, 'frame', 'row'), may hold values from -0.15625 to 0.15625
- timesteps: int32 [2], replicated, may hold values from 0 to 999
- frame_counts: int32 [2], replicated, may hold values from 1 to 4, as said below
- spatial_weight: bfloat16 [4, 9, 320, 320], P('segment'), may hold values from -0.109375 to 0.109375
- temporal_weight: bfloat16 [4, 3, 320, 320], P('segment'), may hold values from -0.1875 to 0.1875
- time_weight: bfloat16 [4, 1280, 320], P('segment'), may hold values from -0.15625 to 0.15625
- norm_gain: float32 [4, 320], P('segment'), may hold values from 0.5 to 1.5
Outputs:
- spatial_grad: float32 [4, 2880, 320], P('segment', ('frame', 'row'))
- temporal_grad: float32 [4, 960, 320], P('segment', ('frame', 'row'))
- time_grad: float32 [4, 1280, 320], P('segment', ('frame', 'row'))
- gain_grad: float32 [4, 320], P('segment', ('frame', 'row'))
The draws below stay inside these ranges and needn't reach their ends.
Inputs may be any that keep to these rules, and one draw needn't show every extreme that they name: Frames frame_counts[c] and later of clip c are padding; some clip has all 4 frames.
All inputs are finite; a program needn't handle non-finite values.
Results may differ from the reference program's by a relative error of at most 0.02.
Values may be sent and summed in bfloat16 or wider, within the bound.
A program may use at most 128 MiB of HBM per device.

```python
import jax
import jax.numpy as jnp
from jax import lax

C = 320
G = 32
TE = 1280
WIDTH = 24
CLIPS = 2
SECTIONS = 4
FRAMES = 4
ROWS = 8


def draw_latents(key, part):
    subkeys = jax.random.split(key, 3)
    full_shape = (CLIPS, FRAMES, ROWS, WIDTH, C)
    frame_pos = jnp.arange(FRAMES).astype(jnp.float32) / max(FRAMES - 1, 1)
    jitter = jnp.exp(jax.random.uniform(subkeys[0], (CLIPS, FRAMES, ROWS, 1, 1), minval=-0.3, maxval=0.3))
    channel_scale = 10.0 ** (jax.random.uniform(subkeys[1], (C,)) - 0.5)
    frame_scale = 10.0 ** (frame_pos - 0.5)
    cell_scale = 0.3 * frame_scale[None, :, None, None, None] * jitter * channel_scale
    values = cell_scale * jax.random.normal(subkeys[2], full_shape)
    return values.astype(jnp.bfloat16)


def draw_frame_counts(key, part):
    subkeys = jax.random.split(key, 2)
    fewest = max(1, FRAMES // 4)
    counts = jax.random.randint(subkeys[0], (CLIPS,), fewest, FRAMES + 1)
    full_clip = jax.random.randint(subkeys[1], (), 0, CLIPS)
    counts = counts.at[full_clip].set(FRAMES)
    return counts.astype(jnp.int32)


def steps_of(key, extent, pieces, low, high):
    def one(position, blocks):
        draws = jax.random.uniform(jax.random.fold_in(jax.random.fold_in(key, 6), position), (blocks,), jnp.float32, low / len(pieces), high / len(pieces))
        return jnp.repeat(jnp.exp(draws), extent[position] // blocks).reshape((-1,) + (1,) * (len(extent) - position - 1))

    level = one(*pieces[0])
    for cut in pieces[1:]:
        level = level * one(*cut)
    return level


def noise(key, dims, width, reach, pieces=(), kind=jnp.bfloat16):
    values = width * jax.random.normal(key, dims, jnp.float32)
    if pieces:
        values = values * steps_of(key, dims, pieces, -0.22, 0.18)
    return jnp.clip(values, -reach, reach).astype(kind)


def setup_inputs(seed: int = 0) -> dict:
    key_list = jax.random.split(jax.random.key(seed), 9)
    return {
        "latents": draw_latents(jax.random.fold_in(key_list[8], 71), 0),
        "cotangent": noise(key_list[1], (CLIPS, FRAMES, ROWS, WIDTH, C), (CLIPS * FRAMES * ROWS * WIDTH) ** -0.5, 0.15625, ((1, 2), (2, 4))),
        "timesteps": jax.random.randint(key_list[2], (CLIPS,), 0, 1000).astype(jnp.int32),
        "frame_counts": draw_frame_counts(jax.random.fold_in(key_list[8], 71), 0),
        "spatial_weight": noise(key_list[4], (SECTIONS, 9, C, C), (9 * C) ** -0.5, 0.109375, ((0, 4),)),
        "temporal_weight": noise(key_list[5], (SECTIONS, 3, C, C), (3 * C) ** -0.5, 0.1875, ((0, 4),)),
        "time_weight": noise(key_list[6], (SECTIONS, TE, C), TE ** -0.5, 0.15625, ((0, 4),)),
        "norm_gain": jnp.clip(0.5 + 1.0 * jax.random.uniform(key_list[7], (SECTIONS, C), jnp.float32) ** steps_of(key_list[7], (SECTIONS, C), ((0, 4),), -0.2, 0.2), 0.5, 1.5),
    }


EPSILON = 1e-05

def time_features(timesteps):
    half_dim = TE // 2
    frequency = jnp.exp(-jnp.log(10000.0) * jnp.arange(half_dim).astype(jnp.float32) / half_dim)
    angles = timesteps.astype(jnp.float32)[:, None] * frequency[None, :]
    wave_parts = jnp.concatenate([jnp.cos(angles), jnp.sin(angles)], axis=1)
    return jax.nn.silu(wave_parts).astype(jnp.bfloat16)

def group_sum(values):
    per_channel = lax.optimization_barrier(jnp.sum(values, axis=(0, 1, 2)))
    return per_channel.reshape(G, -1).sum(axis=1)

def spread(values):
    return jnp.repeat(values, C // G)

def spatial_columns(padded, row_count, col_count):
    return jnp.concatenate([padded[:, vertical:vertical + row_count, lateral:lateral + col_count, :] for vertical in range(3) for lateral in range(3)], axis=-1)

def flip_columns(padded, row_count, col_count):
    return jnp.concatenate([padded[:, 2 - vertical:2 - vertical + row_count, 2 - lateral:2 - lateral + col_count, :] for vertical in range(3) for lateral in range(3)], axis=-1)

def time_columns(padded, frame_count):
    return jnp.concatenate([padded[offset:offset + frame_count] for offset in range(3)], axis=-1)

def time_flip(padded, frame_count):
    return jnp.concatenate([padded[2 - offset:2 - offset + frame_count] for offset in range(3)], axis=-1)

def flat_dot(columns, matrix):
    return jnp.dot(columns.reshape(-1, matrix.shape[0]), matrix, preferred_element_type=jnp.float32)

def outer_dot(columns, right_side):
    return jnp.dot(columns.reshape(-1, columns.shape[-1]).T, right_side.reshape(-1, right_side.shape[-1]), preferred_element_type=jnp.float32)

def section_forward(current, kernel, tkernel, bias_row, gain_row, frame_mask, cell_total):
    frame_count, row_count, col_count, channels = current.shape
    padded_in = jnp.pad(current, ((0, 0), (1, 1), (1, 1), (0, 0)))
    hidden = flat_dot(spatial_columns(padded_in, row_count, col_count), kernel.reshape(9 * channels, channels)).reshape(current.shape) + bias_row
    group_mean = group_sum(hidden * frame_mask) / cell_total
    centred = hidden - spread(group_mean)
    variance = group_sum(frame_mask * centred * centred) / cell_total
    inv_spread = lax.rsqrt(variance + EPSILON)
    normed = centred * spread(inv_spread)
    activated = (frame_mask * jax.nn.silu(normed * gain_row)).astype(jnp.bfloat16)
    padded_act = jnp.pad(activated, ((1, 1), (0, 0), (0, 0), (0, 0)))
    temporal = flat_dot(time_columns(padded_act, frame_count), tkernel.reshape(3 * channels, channels)).reshape(current.shape)
    output = (current.astype(jnp.float32) + temporal).astype(jnp.bfloat16)
    return (output, (padded_in, hidden, padded_act, group_mean, inv_spread))

def section_backward(upstream, stored, kernel, tkernel, gain_row, frame_mask, cell_total):
    padded_in, hidden, padded_act, group_mean, inv_spread = stored
    frame_count, row_count, col_count, channels = hidden.shape
    padded_up = jnp.pad(upstream, ((1, 1), (0, 0), (0, 0), (0, 0)))
    tkernel_back = jnp.transpose(tkernel, (0, 2, 1)).reshape(3 * channels, channels)
    act_grad = flat_dot(time_flip(padded_up, frame_count), tkernel_back).reshape(hidden.shape)
    temporal_part = outer_dot(time_columns(padded_act, frame_count), upstream)
    normed = (hidden - spread(group_mean)) * spread(inv_spread)
    scaled = normed * gain_row
    gate_sig = jax.nn.sigmoid(scaled)
    scaled_grad = act_grad * frame_mask * gate_sig * (1.0 + scaled * (1.0 - gate_sig))
    gain_part = lax.optimization_barrier(jnp.sum(scaled_grad * normed, axis=(0, 1, 2)))
    normed_grad = scaled_grad * gain_row
    first_moment = group_sum(normed_grad) / cell_total
    second_moment = group_sum(normed_grad * normed) / cell_total
    hidden_grad = (spread(inv_spread) * (normed_grad - frame_mask * (spread(first_moment) + normed * spread(second_moment)))).astype(jnp.bfloat16)
    column_sums = lax.optimization_barrier(jnp.sum(hidden_grad.astype(jnp.float32), axis=(0, 1, 2)))
    spatial_part = outer_dot(spatial_columns(padded_in, row_count, col_count), hidden_grad)
    padded_grad = jnp.pad(hidden_grad, ((0, 0), (1, 1), (1, 1), (0, 0)))
    kernel_back = jnp.transpose(kernel, (0, 2, 1)).reshape(9 * channels, channels)
    conv_back = flat_dot(flip_columns(padded_grad, row_count, col_count), kernel_back).reshape(hidden.shape)
    input_grad = (upstream.astype(jnp.float32) + conv_back).astype(jnp.bfloat16)
    return (input_grad, spatial_part, temporal_part, gain_part, column_sums)

def reference(latents, cotangent, timesteps, frame_counts, spatial_weight, temporal_weight, time_weight, norm_gain):
    sections = spatial_weight.shape[0]
    time_embed = time_features(timesteps)
    biases = [jnp.dot(time_embed, time_weight[section], preferred_element_type=jnp.float32) for section in range(sections)]
    frame_ids = jnp.arange(FRAMES).astype(jnp.int32)
    group_width = C // G
    totals = (jnp.zeros((sections, 9 * C, C), jnp.float32), jnp.zeros((sections, 3 * C, C), jnp.float32), jnp.zeros((sections, TE, C), jnp.float32), jnp.zeros((sections, C), jnp.float32))

    def one_clip(totals, clip_index):
        frame_limit = frame_counts[clip_index]
        frame_mask = (frame_ids < frame_limit).astype(jnp.float32)[:, None, None, None]
        cell_total = frame_limit.astype(jnp.float32) * ROWS * WIDTH * group_width
        stored_list = []
        current = latents[clip_index]
        skip_path = current
        for section in range(sections):
            if section == sections - 1:
                current = (current.astype(jnp.float32) + skip_path.astype(jnp.float32)).astype(jnp.bfloat16)
            current, stored = section_forward(current, spatial_weight[section], temporal_weight[section], biases[section][clip_index], norm_gain[section], frame_mask, cell_total)
            stored_list.append(stored)
            if section == 0:
                skip_path = current
        upstream = (frame_mask * cotangent[clip_index].astype(jnp.float32)).astype(jnp.bfloat16)
        skip_grad = upstream
        embed_row = time_embed[clip_index].astype(jnp.float32)
        spatial_total, temporal_total, time_total, gain_total = totals
        for section in reversed(range(sections)):
            if section == 0:
                upstream = (upstream.astype(jnp.float32) + skip_grad.astype(jnp.float32)).astype(jnp.bfloat16)
            input_grad, spatial_part, temporal_part, gain_part, column_sums = section_backward(upstream, stored_list[section], spatial_weight[section], temporal_weight[section], norm_gain[section], frame_mask, cell_total)
            spatial_total = spatial_total.at[section].add(spatial_part)
            temporal_total = temporal_total.at[section].add(temporal_part)
            time_total = time_total.at[section].add(embed_row[:, None] * column_sums[None, :])
            gain_total = gain_total.at[section].add(gain_part)
            if section == sections - 1:
                skip_grad = input_grad
            upstream = input_grad
        return ((spatial_total, temporal_total, time_total, gain_total), None)
    totals, ignored = lax.scan(one_clip, totals, jnp.arange(CLIPS).astype(jnp.int32))
    return (totals[0], totals[1], totals[2], totals[3])
```

```python
import functools

import jax
import jax.numpy as jnp
from jax import lax
from jax.experimental import pallas as pl
from jax.experimental.pallas import tpu as pltpu
from jax.sharding import PartitionSpec as P

C = 320
G = 32
TE = 1280
WIDTH = 24
R_DEV = 2
F_DEV = 2
CLIPS = 2


EPSILON = 1e-05


def time_features(timesteps):
    half_dim = TE // 2
    frequency = jnp.exp(-jnp.log(10000.0) * jnp.arange(half_dim).astype(jnp.float32) / half_dim)
    angles = timesteps.astype(jnp.float32)[:, None] * frequency[None, :]
    wave_parts = jnp.concatenate([jnp.cos(angles), jnp.sin(angles)], axis=1)
    return jax.nn.silu(wave_parts).astype(jnp.bfloat16)


PAD = 32
BLOCK = F_DEV * CLIPS * PAD
CELLS = R_DEV * BLOCK
HALF = CLIPS * PAD
MESH = pl.DeviceIdType.MESH


def swap_order(flat):
    return jnp.concatenate(
        [flat[:HALF], flat[2 * HALF : 3 * HALF], flat[HALF : 2 * HALF], flat[3 * HALF :]], axis=0
    )


def dot_nn(left, right):
    return lax.dot_general(left, right, (((1,), (0,)), ((), ())), preferred_element_type=jnp.float32)


def dot_nt(left, right):
    return lax.dot_general(left, right, (((1,), (1,)), ((), ())), preferred_element_type=jnp.float32)


def widen(padded, wide):
    values = padded[...]
    exact = values.astype(jnp.float32)
    length = values.shape[0]
    wide[0] = pltpu.roll(exact, 1, 0).astype(jnp.bfloat16)
    wide[1] = values
    wide[2] = pltpu.roll(exact, length - 1, 0).astype(jnp.bfloat16)


def section_kernel(
    sections, n_frame, n_row,
    first_x, last_up, bias, mask, width_mask, inv_total, kernel, tkernel, gain, groups,
    spatial_out, temporal_out, sums_out,
    x_in, skip_in, x_out, u_in, u_skip, u_out, pad_x, pad_a, pad_u, pad_h, wide_x, wide_h,
    x_turned, a_turned, normed, grads, stat_src, slots, send_sem, recv_sem,
):
    seg = lax.axis_index("segment")
    frame = lax.axis_index("frame")
    row = lax.axis_index("row")
    peers = n_frame * n_row
    me = frame * n_row + row
    last = sections - 1
    pending = []

    def member(index):
        return (seg, index // n_row, index % n_row)

    def remote(source, target, sem, device):
        return pltpu.make_async_remote_copy(
            src_ref=source,
            dst_ref=target,
            send_sem=send_sem.at[sem],
            recv_sem=recv_sem.at[sem],
            device_id=device,
            device_id_type=MESH,
        )

    def start_if(condition, copy):
        @pl.when(condition)
        def _():
            copy.start()

        pending.append((condition, copy))

    barrier = pltpu.get_barrier_semaphore()

    def greet(device):
        pl.semaphore_signal(barrier, inc=1, device_id=device, device_id_type=MESH)

    for step in range(1, peers):
        greet(member((me + step) % peers))

    @pl.when(seg > 0)
    def _():
        greet((seg - 1, frame, row))

    @pl.when(seg < last)
    def _():
        greet((seg + 1, frame, row))

    @pl.when((seg == 0) | (seg == last))
    def _():
        greet((last - seg, frame, row))

    linked = (seg > 0).astype(jnp.int32) + (seg < last).astype(jnp.int32)
    linked = linked + ((seg == 0) | (seg == last)).astype(jnp.int32)
    pl.semaphore_wait(barrier, peers - 1 + linked)

    after = (jnp.minimum(seg + 1, last), frame, row)
    before = (jnp.maximum(seg - 1, 0), frame, row)
    far = (last - seg, frame, row)
    x_copy = remote(x_out, x_in, 0, after)
    skip_copy = remote(x_out, skip_in, 1, far)
    u_copy = remote(u_out, u_in, 10, before)
    u_skip_copy = remote(u_out, u_skip, 11, far)

    def halo_start(padded, sem, index, size, at):
        onward = remote(
            padded.at[pl.ds(2 * BLOCK, BLOCK)], padded.at[pl.ds(0, BLOCK)],
            sem, at(jnp.minimum(index + 1, size - 1)),
        )
        back = remote(
            padded.at[pl.ds(BLOCK, BLOCK)], padded.at[pl.ds(3 * BLOCK, BLOCK)],
            sem + 1, at(jnp.maximum(index - 1, 0)),
        )
        start_if(index < size - 1, onward)
        start_if(index > 0, back)

        @pl.when(index == 0)
        def _():
            padded[pl.ds(0, BLOCK), :] = jnp.zeros((BLOCK, C), jnp.bfloat16)

        @pl.when(index == size - 1)
        def _():
            padded[pl.ds(3 * BLOCK, BLOCK), :] = jnp.zeros((BLOCK, C), jnp.bfloat16)

        return onward, back, index, size

    def halo_wait(started):
        onward, back, index, size = started

        @pl.when(index > 0)
        def _():
            onward.wait_recv()

        @pl.when(index < size - 1)
        def _():
            back.wait_recv()

    def row_start(padded, sem):
        return halo_start(padded, sem, row, n_row, lambda index: (seg, frame, index))

    def frame_start(padded, sem):
        return halo_start(padded, sem, frame, n_frame, lambda index: (seg, index, row))

    def exchange_start(turn, rows):
        stat_src[turn] = jnp.concatenate(rows + [jnp.zeros((8 - len(rows), C), jnp.float32)], axis=0)
        copies = []
        for step in range(1, peers):
            copy = remote(
                stat_src.at[turn], slots.at[turn, step - 1],
                12 + turn * (peers - 1) + step - 1, member((me + step) % peers),
            )
            copy.start()
            pending.append((None, copy))
            copies.append(copy)
        return turn, copies

    def exchange_wait(started):
        turn, copies = started
        total = stat_src[turn]
        for step, copy in enumerate(copies):
            copy.wait_recv()
            total = total + slots[turn, step]
        return total

    def column_sum(values):
        return jnp.sum(values.reshape(-1, C), axis=0, keepdims=True)

    def grouped(total):
        return lax.dot_general(
            total * inv_total[...], groups[...], (((1,), (0,)), ((), ())),
            precision=lax.Precision.HIGHEST, preferred_element_type=jnp.float32,
        )

    own = pl.ds(BLOCK, CELLS)

    @pl.when(seg == 0)
    def _():
        pad_x[own, :] = first_x[...]

    @pl.when(seg > 0)
    def _():
        x_copy.wait_recv()

    @pl.when((seg > 0) & (seg < last))
    def _():
        pad_x[own, :] = x_in[...]

    @pl.when(seg == last)
    def _():
        skip_copy.wait_recv()
        joined = x_in[...].astype(jnp.float32) + skip_in[...].astype(jnp.float32)
        pad_x[own, :] = joined.astype(jnp.bfloat16)

    halo_wait(row_start(pad_x, 2))
    widen(pad_x, wide_x)
    hidden = jnp.zeros((CELLS, C), jnp.float32)
    for a in range(3):
        for b in range(3):
            hidden = hidden + dot_nn(wide_x[b, pl.ds(a * BLOCK, CELLS), :], kernel[3 * a + b])
    normed[...] = hidden.reshape(normed.shape)
    rows = []
    for clip in range(CLIPS):
        part = normed[:, clip] + bias[pl.ds(clip, 1), :].reshape(1, 1, C)
        normed[:, clip] = part
        masked = part * mask[:, clip]
        rows += [column_sum(masked), column_sum(masked * part)]
    stats = exchange_start(0, rows)
    for b in range(3):
        x_turned[b] = jnp.transpose(wide_x[b], (1, 0))
    stats = grouped(exchange_wait(stats))
    inverses = []
    for clip in range(CLIPS):
        mean = stats[2 * clip : 2 * clip + 1]
        variance = stats[2 * clip + 1 : 2 * clip + 2] - mean * mean
        inverse = lax.rsqrt(variance + EPSILON)
        inverses.append(inverse)
        part = (normed[:, clip] - mean.reshape(1, 1, C)) * inverse.reshape(1, 1, C)
        normed[:, clip] = part
        scaled = part * gain[...].reshape(1, 1, C)
        grads[:, clip] = mask[:, clip] * (scaled * jax.nn.sigmoid(scaled))
    pad_a[own, :] = swap_order(grads[...].reshape(CELLS, C)).astype(jnp.bfloat16)
    halo_wait(frame_start(pad_a, 4))
    temporal = jnp.zeros((CELLS, C), jnp.float32)
    for k in range(3):
        temporal = temporal + dot_nn(pad_a[pl.ds(k * BLOCK, CELLS), :], tkernel[k])

    @pl.when(seg < last)
    def _():
        x_out[...] = (pad_x[own, :].astype(jnp.float32) + swap_order(temporal)).astype(jnp.bfloat16)

    start_if(seg < last, x_copy)
    start_if(seg == 0, skip_copy)
    a_turned[...] = jnp.transpose(pad_a[...], (1, 0))

    @pl.when(seg == last)
    def _():
        pad_u[own, :] = swap_order(last_up[...])

    @pl.when(seg < last)
    def _():
        u_copy.wait_recv()

    @pl.when((seg > 0) & (seg < last))
    def _():
        pad_u[own, :] = swap_order(u_in[...])

    @pl.when(seg == 0)
    def _():
        u_skip_copy.wait_recv()
        joined = u_in[...].astype(jnp.float32) + u_skip[...].astype(jnp.float32)
        pad_u[own, :] = swap_order(joined.astype(jnp.bfloat16))

    halo_wait(frame_start(pad_u, 6))
    act_grad = jnp.zeros((CELLS, C), jnp.float32)
    for k in range(3):
        act_grad = act_grad + dot_nt(pad_u[pl.ds((2 - k) * BLOCK, CELLS), :], tkernel[k])
    grads[...] = swap_order(act_grad).reshape(grads.shape)
    rows = []
    gain_part = jnp.zeros((1, C), jnp.float32)
    for clip in range(CLIPS):
        part = normed[:, clip]
        scaled = part * gain[...].reshape(1, 1, C)
        gate = jax.nn.sigmoid(scaled)
        scaled_grad = grads[:, clip] * mask[:, clip] * gate * (1.0 + scaled * (1.0 - gate))
        gain_part = gain_part + column_sum(scaled_grad * part)
        normed_grad = scaled_grad * gain[...].reshape(1, 1, C)
        grads[:, clip] = normed_grad
        rows += [column_sum(normed_grad), column_sum(normed_grad * part)]
    moments = exchange_start(1, rows)
    for k in range(3):
        temporal_out[k] = dot_nn(a_turned[:, pl.ds(k * BLOCK, CELLS)], pad_u[own, :])
    moments = grouped(exchange_wait(moments))
    rows = []
    for clip in range(CLIPS):
        first = moments[2 * clip : 2 * clip + 1].reshape(1, 1, C)
        second = moments[2 * clip + 1 : 2 * clip + 2].reshape(1, 1, C)
        part = inverses[clip].reshape(1, 1, C) * (
            grads[:, clip] - mask[:, clip] * (first + normed[:, clip] * second)
        )
        part = part.astype(jnp.bfloat16).astype(jnp.float32)
        grads[:, clip] = part
        rows.append(column_sum(part))
    pad_h[own, :] = grads[...].reshape(CELLS, C).astype(jnp.bfloat16)
    sums = exchange_start(2, rows + [gain_part])

    @pl.when(seg > 0)
    def _():
        halo = []
        pending_before = len(pending)
        halo = row_start(pad_h, 8)
        halo_wait(halo)
        widen(pad_h, wide_h)
        back = jnp.zeros((CELLS, C), jnp.float32)
        for a in range(3):
            for b in range(3):
                back = back + dot_nt(
                    wide_h[2 - b, pl.ds((2 - a) * BLOCK, CELLS), :], kernel[3 * a + b]
                )
        upstream = swap_order(pad_u[own, :]).astype(jnp.float32)
        u_out[...] = (upstream + back * width_mask[...]).astype(jnp.bfloat16)
        u_copy.start()
        for condition, copy in pending[pending_before:]:
            pl.when(condition)(copy.wait_send)
        del pending[pending_before:]

    @pl.when(seg == last)
    def _():
        u_skip_copy.start()

    for a in range(3):
        for b in range(3):
            spatial_out[3 * a + b] = dot_nn(
                x_turned[b, :, pl.ds(a * BLOCK, CELLS)], pad_h[own, :]
            )
    sums_out[...] = exchange_wait(sums)
    for condition, copy in pending + [(seg > 0, u_copy), (seg == last, u_skip_copy)]:
        if condition is None:
            copy.wait_send()
        else:
            pl.when(condition)(copy.wait_send)


def run_section(sections, n_frame, n_row, *operands):
    peers = n_frame * n_row
    flat = pltpu.VMEM((CELLS, C), jnp.bfloat16)
    padded = pltpu.VMEM((2 * CELLS, C), jnp.bfloat16)
    field = pltpu.VMEM((R_DEV * F_DEV, CLIPS, PAD, C), jnp.float32)
    sems = 12 + 3 * (peers - 1)
    vmem = pl.BlockSpec(memory_space=pltpu.VMEM)
    return pl.pallas_call(
        functools.partial(section_kernel, sections, n_frame, n_row),
        out_shape=(
            jax.ShapeDtypeStruct((9, C, C), jnp.float32),
            jax.ShapeDtypeStruct((3, C, C), jnp.float32),
            jax.ShapeDtypeStruct((8, C), jnp.float32),
        ),
        in_specs=[vmem] * len(operands),
        out_specs=(vmem, vmem, vmem),
        scratch_shapes=[flat] * 6
        + [padded] * 4
        + [pltpu.VMEM((3, 2 * CELLS, C), jnp.bfloat16)] * 2
        + [
            pltpu.VMEM((3, C, 2 * CELLS), jnp.bfloat16),
            pltpu.VMEM((C, 2 * CELLS), jnp.bfloat16),
            field,
            field,
            pltpu.VMEM((3, 8, C), jnp.float32),
            pltpu.VMEM((3, peers - 1, 8, C), jnp.float32),
            pltpu.SemaphoreType.DMA((sems,)),
            pltpu.SemaphoreType.DMA((sems,)),
        ],
        compiler_params=pltpu.CompilerParams(
            collective_id=0, has_side_effects=True, vmem_limit_bytes=48 * 1024 * 1024
        ),
    )(*operands)


def to_cells(array):
    turned = jnp.transpose(array, (2, 1, 0, 3, 4))
    turned = jnp.pad(turned, ((0, 0), (0, 0), (0, 0), (0, PAD - WIDTH), (0, 0)))
    return turned.reshape(CELLS, C)


def per_device(
    latents,
    cotangent,
    timesteps,
    frame_counts,
    spatial_weight,
    temporal_weight,
    time_weight,
    norm_gain,
):
    sections = lax.axis_size("segment")
    n_frame = lax.axis_size("frame")
    n_row = lax.axis_size("row")
    peers = n_frame * n_row
    me = lax.axis_index("frame") * n_row + lax.axis_index("row")
    group_width = C // G
    time_embed = time_features(timesteps)
    biases = jnp.dot(time_embed, time_weight[0], preferred_element_type=jnp.float32)
    frame_ids = lax.axis_index("frame") * F_DEV + jnp.arange(F_DEV)
    frame_mask = (frame_ids[None, :] < frame_counts[:, None]).astype(jnp.float32)
    upstream = (frame_mask[:, :, None, None, None] * cotangent.astype(jnp.float32)).astype(jnp.bfloat16)
    inside = (jnp.arange(PAD) < WIDTH).astype(jnp.float32)
    cell_mask = frame_mask.T[None, :, :, None] * inside
    cell_mask = jnp.broadcast_to(cell_mask, (R_DEV, F_DEV, CLIPS, PAD))
    width_mask = jnp.broadcast_to(inside, (R_DEV, F_DEV, CLIPS, PAD)).reshape(CELLS, 1)
    totals = frame_counts.astype(jnp.float32) * (R_DEV * n_row) * WIDTH * group_width
    inv_total = jnp.pad(jnp.repeat(1.0 / totals, 2), (0, 8 - 2 * CLIPS))[:, None]
    channel_group = jnp.arange(C) // group_width
    groups = (channel_group[:, None] == channel_group[None, :]).astype(jnp.float32)
    spatial, temporal, sums = run_section(
        sections,
        n_frame,
        n_row,
        to_cells(latents),
        to_cells(upstream),
        biases,
        cell_mask.reshape(R_DEV * F_DEV, CLIPS, PAD, 1),
        width_mask,
        inv_total,
        spatial_weight[0],
        temporal_weight[0],
        norm_gain,
        groups,
    )
    parts = jnp.concatenate(
        [spatial.reshape(peers, -1, C), temporal.reshape(peers, -1, C)], axis=1
    ).astype(jnp.bfloat16)
    reduced = lax.psum_scatter(parts, ("frame", "row"), scatter_dimension=0, tiled=True)[0]
    reduced = reduced.astype(jnp.float32)
    spatial_rows = 9 * C // peers
    time_rows = TE // peers
    embed = lax.dynamic_slice_in_dim(time_embed, me * time_rows, time_rows, 1).astype(jnp.float32)
    time_out = embed[0][:, None] * sums[0][None, :]
    for clip in range(1, CLIPS):
        time_out = time_out + embed[clip][:, None] * sums[clip][None, :]
    gain_out = lax.dynamic_slice_in_dim(sums[CLIPS], me * (C // peers), C // peers, 0)
    return (reduced[:spatial_rows][None], reduced[spatial_rows:][None], time_out[None], gain_out[None])


def solution(mesh):
    return jax.shard_map(
        per_device,
        mesh=mesh,
        in_specs=(
            P(None, "frame", "row", None, None),
            P(None, "frame", "row", None, None),
            P(),
            P(),
            P("segment", None, None, None),
            P("segment", None, None, None),
            P("segment", None, None),
            P("segment", None),
        ),
        out_specs=(
            P("segment", ("frame", "row"), None),
            P("segment", ("frame", "row"), None),
            P("segment", ("frame", "row"), None),
            P("segment", ("frame", "row")),
        ),
        check_vma=False,
    )
```

```python
import functools

import jax
import jax.numpy as jnp
from jax import lax
from jax.experimental import pallas as pl
from jax.experimental.pallas import tpu as pltpu
from jax.sharding import PartitionSpec as P

C = 320
G = 32
TE = 1280
WIDTH = 24
R_DEV = 2
F_DEV = 2
CLIPS = 2


EPSILON = 1e-05


def time_features(timesteps):
    half_dim = TE // 2
    frequency = jnp.exp(-jnp.log(10000.0) * jnp.arange(half_dim).astype(jnp.float32) / half_dim)
    angles = timesteps.astype(jnp.float32)[:, None] * frequency[None, :]
    wave_parts = jnp.concatenate([jnp.cos(angles), jnp.sin(angles)], axis=1)
    return jax.nn.silu(wave_parts).astype(jnp.bfloat16)


PAD = 32
BLOCK = F_DEV * CLIPS * PAD
CELLS = R_DEV * BLOCK
HALF = CLIPS * PAD
MESH = pl.DeviceIdType.MESH


def swap_order(flat):
    return jnp.concatenate(
        [flat[:HALF], flat[2 * HALF : 3 * HALF], flat[HALF : 2 * HALF], flat[3 * HALF :]], axis=0
    )


def dot_nn(left, right):
    return lax.dot_general(left, right, (((1,), (0,)), ((), ())), preferred_element_type=jnp.float32)


def dot_nt(left, right):
    return lax.dot_general(left, right, (((1,), (1,)), ((), ())), preferred_element_type=jnp.float32)


def widen(padded, wide):
    values = padded[...]
    exact = values.astype(jnp.float32)
    length = values.shape[0]
    wide[0] = pltpu.roll(exact, 1, 0).astype(jnp.bfloat16)
    wide[1] = values
    wide[2] = pltpu.roll(exact, length - 1, 0).astype(jnp.bfloat16)


def section_kernel(
    sections, n_frame, n_row,
    counts, latents, cotangent, embed, kernel, tkernel, time_kernel, gain,
    spatial_out, temporal_out, sums_out,
    x_in, skip_in, x_out, u_in, u_skip, u_out, pad_x, pad_a, pad_u, pad_h, wide_x, wide_h,
    x_turned, a_turned, normed, grads, stat_src, slots, mask, width_mask, groups, bias,
    send_sem, recv_sem, *reduction,
):
    seg = lax.axis_index("segment")
    frame = lax.axis_index("frame")
    row = lax.axis_index("row")
    peers = n_frame * n_row
    me = frame * n_row + row
    last = sections - 1
    pending = []

    def member(index):
        return (seg, index // n_row, index % n_row)

    def remote(source, target, sem, device):
        return pltpu.make_async_remote_copy(
            src_ref=source,
            dst_ref=target,
            send_sem=send_sem.at[sem],
            recv_sem=recv_sem.at[sem],
            device_id=device,
            device_id_type=MESH,
        )

    def start_if(condition, copy):
        @pl.when(condition)
        def _():
            copy.start()

        pending.append((condition, copy))

    place = lax.broadcasted_iota(jnp.int32, (R_DEV * F_DEV, PAD, 1), 0) % F_DEV + frame * F_DEV
    column = lax.broadcasted_iota(jnp.int32, (R_DEV * F_DEV, PAD, 1), 1)
    for clip in range(CLIPS):
        live = (place < counts[clip]) & (column < WIDTH)
        mask[:, clip] = jnp.where(live, 1.0, 0.0)
    column = lax.broadcasted_iota(jnp.int32, (CELLS // PAD, PAD, 1), 1)
    width_mask[...] = jnp.where(column < WIDTH, 1.0, 0.0).reshape(CELLS, 1)
    ids = [lax.broadcasted_iota(jnp.int32, (C, C), dim).astype(jnp.float32) for dim in range(2)]
    ids = [jnp.floor((one + 0.5) * (G / C)) for one in ids]
    groups[...] = jnp.where(ids[0] == ids[1], 1.0, 0.0)
    bias[...] = dot_nn(embed[...], time_kernel[...])
    line = lax.broadcasted_iota(jnp.int32, (8, C), 0)
    in_use = jnp.where(line < 2, counts[0], counts[1]).astype(jnp.float32)
    inv_total = 1.0 / (in_use * (R_DEV * n_row * WIDTH * (C // G)))

    barrier = pltpu.get_barrier_semaphore()

    def greet(device):
        pl.semaphore_signal(barrier, inc=1, device_id=device, device_id_type=MESH)

    for step in range(1, peers):
        greet(member((me + step) % peers))

    @pl.when(seg > 0)
    def _():
        greet((seg - 1, frame, row))

    @pl.when(seg < last)
    def _():
        greet((seg + 1, frame, row))

    @pl.when((seg == 0) | (seg == last))
    def _():
        greet((last - seg, frame, row))

    linked = (seg > 0).astype(jnp.int32) + (seg < last).astype(jnp.int32)
    linked = linked + ((seg == 0) | (seg == last)).astype(jnp.int32)
    pl.semaphore_wait(barrier, peers - 1 + linked)

    after = (jnp.minimum(seg + 1, last), frame, row)
    before = (jnp.maximum(seg - 1, 0), frame, row)
    far = (last - seg, frame, row)
    x_copy = remote(x_out, x_in, 0, after)
    skip_copy = remote(x_out, skip_in, 1, far)
    u_copy = remote(u_out, u_in, 10, before)
    u_skip_copy = remote(u_out, u_skip, 11, far)

    def halo_start(padded, sem, index, size, at):
        onward = remote(
            padded.at[pl.ds(2 * BLOCK, BLOCK)], padded.at[pl.ds(0, BLOCK)],
            sem, at(jnp.minimum(index + 1, size - 1)),
        )
        back = remote(
            padded.at[pl.ds(BLOCK, BLOCK)], padded.at[pl.ds(3 * BLOCK, BLOCK)],
            sem + 1, at(jnp.maximum(index - 1, 0)),
        )
        start_if(index < size - 1, onward)
        start_if(index > 0, back)

        @pl.when(index == 0)
        def _():
            padded[pl.ds(0, BLOCK), :] = jnp.zeros((BLOCK, C), jnp.bfloat16)

        @pl.when(index == size - 1)
        def _():
            padded[pl.ds(3 * BLOCK, BLOCK), :] = jnp.zeros((BLOCK, C), jnp.bfloat16)

        return onward, back, index, size

    def halo_wait(started):
        onward, back, index, size = started

        @pl.when(index > 0)
        def _():
            onward.wait_recv()

        @pl.when(index < size - 1)
        def _():
            back.wait_recv()

    def row_start(padded, sem):
        return halo_start(padded, sem, row, n_row, lambda index: (seg, frame, index))

    def frame_start(padded, sem):
        return halo_start(padded, sem, frame, n_frame, lambda index: (seg, index, row))

    def exchange_start(turn, rows):
        stat_src[turn] = jnp.concatenate(rows + [jnp.zeros((8 - len(rows), C), jnp.float32)], axis=0)
        copies = []
        for step in range(1, peers):
            copy = remote(
                stat_src.at[turn], slots.at[turn, step - 1],
                12 + turn * (peers - 1) + step - 1, member((me + step) % peers),
            )
            copy.start()
            pending.append((None, copy))
            copies.append(copy)
        return turn, copies

    def exchange_wait(started):
        turn, copies = started
        total = stat_src[turn]
        for step, copy in enumerate(copies):
            copy.wait_recv()
            total = total + slots[turn, step]
        return total

    def column_sum(values):
        return jnp.sum(values.reshape(-1, C), axis=0, keepdims=True)

    def grouped(total):
        return lax.dot_general(
            total * inv_total, groups[...], (((1,), (0,)), ((), ())),
            precision=lax.Precision.HIGHEST, preferred_element_type=jnp.float32,
        )

    fused = bool(reduction)
    temporal_sum, spatial_sum = reduction[:2] if fused else (temporal_out, spatial_out)
    first_sem = 12 + 3 * (peers - 1)

    def stage(total, buffers):
        staged = buffers[0]
        rows = total.shape[0] // peers
        for index in range(peers):
            staged[index, :rows] = total[pl.ds(index * rows, rows), :].astype(jnp.bfloat16)
            if rows < staged.shape[1]:
                rest = staged.shape[1] - rows
                staged[index, rows:] = jnp.zeros((rest, C), jnp.bfloat16)

    def pair_start(buffers, turn):
        staged, landed = buffers[:2]
        other = 1 - frame
        copy = remote(
            staged.at[pl.ds(other * n_row, n_row)], landed,
            first_sem + turn * n_row, (seg, other, row),
        )
        copy.start()
        pending.append((None, copy))
        return copy

    def line_start(buffers, turn, pair):
        staged, landed, added, arrived = buffers
        pair.wait_recv()
        copies = []
        for step in range(n_row - 1, 0, -1):
            target = (row + step) % n_row
            mine = staged[frame * n_row + target].astype(jnp.float32)
            added[target] = (mine + landed[target].astype(jnp.float32)).astype(jnp.bfloat16)
            copy = remote(
                added.at[target], arrived.at[step - 1],
                first_sem + turn * n_row + step, (seg, frame, target),
            )
            copy.start()
            pending.append((None, copy))
            copies.append((step, copy))
        return copies

    def line_finish(buffers, copies, result):
        staged, landed, added, arrived = buffers
        total = staged[frame * n_row + row].astype(jnp.float32) + landed[row].astype(jnp.float32)
        for step, copy in copies:
            copy.wait_recv()
            total = total + arrived[step - 1].astype(jnp.float32)
        result[...] = total[: result.shape[0]]

    own = pl.ds(BLOCK, CELLS)

    @pl.when(seg == 0)
    def _():
        pad_x[own, :] = jnp.zeros((CELLS, C), jnp.bfloat16)
        for r in range(R_DEV):
            for f in range(F_DEV):
                for clip in range(CLIPS):
                    start = BLOCK + ((r * F_DEV + f) * CLIPS + clip) * PAD
                    pad_x[pl.ds(start, WIDTH), :] = latents[clip, f, r]

    @pl.when(seg > 0)
    def _():
        x_copy.wait_recv()

    @pl.when((seg > 0) & (seg < last))
    def _():
        pad_x[own, :] = x_in[...]

    @pl.when(seg == last)
    def _():
        skip_copy.wait_recv()
        joined = x_in[...].astype(jnp.float32) + skip_in[...].astype(jnp.float32)
        pad_x[own, :] = joined.astype(jnp.bfloat16)

    halo_wait(row_start(pad_x, 2))
    widen(pad_x, wide_x)
    hidden = jnp.zeros((CELLS, C), jnp.float32)
    for a in range(3):
        for b in range(3):
            hidden = hidden + dot_nn(wide_x[b, pl.ds(a * BLOCK, CELLS), :], kernel[3 * a + b])
    normed[...] = hidden.reshape(normed.shape)
    rows = []
    for clip in range(CLIPS):
        part = normed[:, clip] + bias[pl.ds(clip, 1), :].reshape(1, 1, C)
        normed[:, clip] = part
        masked = part * mask[:, clip]
        rows += [column_sum(masked), column_sum(masked * part)]
    stats = exchange_start(0, rows)
    for b in range(3):
        x_turned[b] = jnp.transpose(wide_x[b], (1, 0))
    stats = grouped(exchange_wait(stats))
    inverses = []
    for clip in range(CLIPS):
        mean = stats[2 * clip : 2 * clip + 1]
        variance = stats[2 * clip + 1 : 2 * clip + 2] - mean * mean
        inverse = lax.rsqrt(variance + EPSILON)
        inverses.append(inverse)
        part = (normed[:, clip] - mean.reshape(1, 1, C)) * inverse.reshape(1, 1, C)
        normed[:, clip] = part
        scaled = part * gain[...].reshape(1, 1, C)
        grads[:, clip] = mask[:, clip] * (scaled * jax.nn.sigmoid(scaled))
    pad_a[own, :] = swap_order(grads[...].reshape(CELLS, C)).astype(jnp.bfloat16)
    halo_wait(frame_start(pad_a, 4))
    temporal = jnp.zeros((CELLS, C), jnp.float32)
    for k in range(3):
        temporal = temporal + dot_nn(pad_a[pl.ds(k * BLOCK, CELLS), :], tkernel[k])

    @pl.when(seg < last)
    def _():
        x_out[...] = (pad_x[own, :].astype(jnp.float32) + swap_order(temporal)).astype(jnp.bfloat16)

    start_if(seg < last, x_copy)
    start_if(seg == 0, skip_copy)
    a_turned[...] = jnp.transpose(pad_a[...], (1, 0))

    @pl.when(seg == last)
    def _():
        pad_u[own, :] = jnp.zeros((CELLS, C), jnp.bfloat16)
        for r in range(R_DEV):
            for f in range(F_DEV):
                for clip in range(CLIPS):
                    start = BLOCK + ((f * R_DEV + r) * CLIPS + clip) * PAD
                    kept = mask[r * F_DEV + f, clip][:WIDTH]
                    value = kept * cotangent[clip, f, r].astype(jnp.float32)
                    pad_u[pl.ds(start, WIDTH), :] = value.astype(jnp.bfloat16)

    @pl.when(seg < last)
    def _():
        u_copy.wait_recv()

    @pl.when((seg > 0) & (seg < last))
    def _():
        pad_u[own, :] = swap_order(u_in[...])

    @pl.when(seg == 0)
    def _():
        u_skip_copy.wait_recv()
        joined = u_in[...].astype(jnp.float32) + u_skip[...].astype(jnp.float32)
        pad_u[own, :] = swap_order(joined.astype(jnp.bfloat16))

    halo_wait(frame_start(pad_u, 6))
    act_grad = jnp.zeros((CELLS, C), jnp.float32)
    for k in range(3):
        act_grad = act_grad + dot_nt(pad_u[pl.ds((2 - k) * BLOCK, CELLS), :], tkernel[k])
    grads[...] = swap_order(act_grad).reshape(grads.shape)
    rows = []
    gain_part = jnp.zeros((1, C), jnp.float32)
    for clip in range(CLIPS):
        part = normed[:, clip]
        scaled = part * gain[...].reshape(1, 1, C)
        gate = jax.nn.sigmoid(scaled)
        scaled_grad = grads[:, clip] * mask[:, clip] * gate * (1.0 + scaled * (1.0 - gate))
        gain_part = gain_part + column_sum(scaled_grad * part)
        normed_grad = scaled_grad * gain[...].reshape(1, 1, C)
        grads[:, clip] = normed_grad
        rows += [column_sum(normed_grad), column_sum(normed_grad * part)]
    moments = exchange_start(1, rows)
    for k in range(3):
        temporal_sum[pl.ds(k * C, C), :] = dot_nn(
            a_turned[:, pl.ds(k * BLOCK, CELLS)], pad_u[own, :]
        )
    if fused:
        stage(temporal_sum, reduction[2:6])
    moments = grouped(exchange_wait(moments))
    if fused:
        temporal_pair = pair_start(reduction[2:6], 0)
    rows = []
    for clip in range(CLIPS):
        first = moments[2 * clip : 2 * clip + 1].reshape(1, 1, C)
        second = moments[2 * clip + 1 : 2 * clip + 2].reshape(1, 1, C)
        part = inverses[clip].reshape(1, 1, C) * (
            grads[:, clip] - mask[:, clip] * (first + normed[:, clip] * second)
        )
        part = part.astype(jnp.bfloat16).astype(jnp.float32)
        grads[:, clip] = part
        rows.append(column_sum(part))
    pad_h[own, :] = grads[...].reshape(CELLS, C).astype(jnp.bfloat16)
    sums = exchange_start(2, rows + [gain_part])

    @pl.when(seg > 0)
    def _():
        halo = []
        pending_before = len(pending)
        halo = row_start(pad_h, 8)
        halo_wait(halo)
        widen(pad_h, wide_h)
        back = jnp.zeros((CELLS, C), jnp.float32)
        for a in range(3):
            for b in range(3):
                back = back + dot_nt(
                    wide_h[2 - b, pl.ds((2 - a) * BLOCK, CELLS), :], kernel[3 * a + b]
                )
        upstream = swap_order(pad_u[own, :]).astype(jnp.float32)
        u_out[...] = (upstream + back * width_mask[...]).astype(jnp.bfloat16)
        u_copy.start()
        for condition, copy in pending[pending_before:]:
            pl.when(condition)(copy.wait_send)
        del pending[pending_before:]

    @pl.when(seg == last)
    def _():
        u_skip_copy.start()

    if fused:
        temporal_line = line_start(reduction[2:6], 0, temporal_pair)
    for a in range(3):
        for b in range(3):
            spatial_sum[pl.ds((3 * a + b) * C, C), :] = dot_nn(
                x_turned[b, :, pl.ds(a * BLOCK, CELLS)], pad_h[own, :]
            )
    if fused:
        stage(spatial_sum, reduction[6:10])
        spatial_line = line_start(reduction[6:10], 1, pair_start(reduction[6:10], 1))
        line_finish(reduction[2:6], temporal_line, temporal_out)
        line_finish(reduction[6:10], spatial_line, spatial_out)
    sums_out[...] = exchange_wait(sums)
    for condition, copy in pending + [(seg > 0, u_copy), (seg == last, u_skip_copy)]:
        if condition is None:
            copy.wait_send()
        else:
            pl.when(condition)(copy.wait_send)


def run_section(sections, n_frame, n_row, *operands):
    peers = n_frame * n_row
    fused = n_frame == 2 and C * 3 % (8 * peers) == 0
    flat = pltpu.VMEM((CELLS, C), jnp.bfloat16)
    padded = pltpu.VMEM((2 * CELLS, C), jnp.bfloat16)
    field = pltpu.VMEM((R_DEV * F_DEV, CLIPS, PAD, C), jnp.float32)
    sems = 12 + 3 * (peers - 1) + 2 * n_row
    vmem = pl.BlockSpec(memory_space=pltpu.VMEM)
    smem = pl.BlockSpec(memory_space=pltpu.SMEM)
    taps = (3, 9)
    share = peers if fused else 1
    reduction = []
    if fused:
        reduction = [pltpu.VMEM((count * C, C), jnp.float32) for count in taps]
        for count in taps:
            rows = -(-count * C // (16 * peers)) * 16
            reduction += [
                pltpu.VMEM((held, rows, C), jnp.bfloat16) for held in (peers, n_row, n_row, n_row - 1)
            ]
    return pl.pallas_call(
        functools.partial(section_kernel, sections, n_frame, n_row),
        out_shape=(
            jax.ShapeDtypeStruct((9 * C // share, C), jnp.float32),
            jax.ShapeDtypeStruct((3 * C // share, C), jnp.float32),
            jax.ShapeDtypeStruct((8, C), jnp.float32),
        ),
        in_specs=[smem] + [vmem] * (len(operands) - 1),
        out_specs=(vmem, vmem, vmem),
        scratch_shapes=[flat] * 6
        + [padded] * 4
        + [pltpu.VMEM((3, 2 * CELLS, C), jnp.bfloat16)] * 2
        + [
            pltpu.VMEM((3, C, 2 * CELLS), jnp.bfloat16),
            pltpu.VMEM((C, 2 * CELLS), jnp.bfloat16),
            field,
            field,
            pltpu.VMEM((3, 8, C), jnp.float32),
            pltpu.VMEM((3, peers - 1, 8, C), jnp.float32),
            pltpu.VMEM((R_DEV * F_DEV, CLIPS, PAD, 1), jnp.float32),
            pltpu.VMEM((CELLS, 1), jnp.float32),
            pltpu.VMEM((C, C), jnp.float32),
            pltpu.VMEM((16, C), jnp.float32),
            pltpu.SemaphoreType.DMA((sems,)),
            pltpu.SemaphoreType.DMA((sems,)),
        ]
        + reduction,
        compiler_params=pltpu.CompilerParams(
            collective_id=0, has_side_effects=True, vmem_limit_bytes=56 * 1024 * 1024
        ),
    )(*operands)


def per_device(
    latents,
    cotangent,
    timesteps,
    frame_counts,
    spatial_weight,
    temporal_weight,
    time_weight,
    norm_gain,
):
    sections = lax.axis_size("segment")
    n_frame = lax.axis_size("frame")
    n_row = lax.axis_size("row")
    peers = n_frame * n_row
    me = lax.axis_index("frame") * n_row + lax.axis_index("row")
    time_embed = time_features(jnp.pad(timesteps, (0, 16 - CLIPS)))
    spatial, temporal, sums = run_section(
        sections,
        n_frame,
        n_row,
        frame_counts,
        latents,
        cotangent,
        time_embed,
        spatial_weight[0],
        temporal_weight[0],
        time_weight[0],
        norm_gain,
    )
    if spatial.shape[0] == 9 * C:
        parts = [spatial.reshape(peers, -1, C), temporal.reshape(peers, -1, C)]
        parts = jnp.concatenate(parts, axis=1).astype(jnp.bfloat16)
        reduced = lax.psum_scatter(parts, ("frame", "row"), scatter_dimension=0, tiled=True)[0]
        reduced = reduced.astype(jnp.float32)
        spatial, temporal = reduced[: 9 * C // peers], reduced[9 * C // peers :]
    time_rows = TE // peers
    embed = lax.dynamic_slice_in_dim(time_embed, me * time_rows, time_rows, 1).astype(jnp.float32)
    time_out = embed[0][:, None] * sums[0][None, :]
    for clip in range(1, CLIPS):
        time_out = time_out + embed[clip][:, None] * sums[clip][None, :]
    gain_out = lax.dynamic_slice_in_dim(sums[CLIPS], me * (C // peers), C // peers, 0)
    return (spatial[None], temporal[None], time_out[None], gain_out[None])


def solution(mesh):
    return jax.shard_map(
        per_device,
        mesh=mesh,
        in_specs=(
            P(None, "frame", "row", None, None),
            P(None, "frame", "row", None, None),
            P(),
            P(),
            P("segment", None, None, None),
            P("segment", None, None, None),
            P("segment", None, None),
            P("segment", None),
        ),
        out_specs=(
            P("segment", ("frame", "row"), None),
            P("segment", ("frame", "row"), None),
            P("segment", ("frame", "row"), None),
            P("segment", ("frame", "row")),
        ),
        check_vma=False,
    )
```

```python
import functools

import jax
import jax.numpy as jnp
from jax import lax
from jax.experimental import pallas as pl
from jax.experimental.pallas import tpu as pltpu
from jax.sharding import PartitionSpec as P

C = 320
G = 32
TE = 1280
WIDTH = 24
R_DEV = 2
F_DEV = 2
CLIPS = 2


EPSILON = 1e-05


def time_features(timesteps):
    half_dim = TE // 2
    frequency = jnp.exp(-jnp.log(10000.0) * jnp.arange(half_dim).astype(jnp.float32) / half_dim)
    angles = timesteps.astype(jnp.float32)[:, None] * frequency[None, :]
    wave_parts = jnp.concatenate([jnp.cos(angles), jnp.sin(angles)], axis=1)
    return jax.nn.silu(wave_parts).astype(jnp.bfloat16)


PAD = 32
BLOCK = F_DEV * CLIPS * PAD
CELLS = R_DEV * BLOCK
HALF = CLIPS * PAD
MESH = pl.DeviceIdType.MESH


def swap_order(flat):
    return jnp.concatenate(
        [flat[:HALF], flat[2 * HALF : 3 * HALF], flat[HALF : 2 * HALF], flat[3 * HALF :]], axis=0
    )


def dot_nn(left, right):
    return lax.dot_general(left, right, (((1,), (0,)), ((), ())), preferred_element_type=jnp.float32)


def dot_nt(left, right):
    return lax.dot_general(left, right, (((1,), (1,)), ((), ())), preferred_element_type=jnp.float32)


def widen(padded, wide, start, length):
    some = pl.ds(start, length)
    values = padded[some, :]
    exact = values.astype(jnp.float32)
    wide[0, some, :] = pltpu.roll(exact, 1, 0).astype(jnp.bfloat16)
    wide[1, some, :] = values
    wide[2, some, :] = pltpu.roll(exact, length - 1, 0).astype(jnp.bfloat16)


def section_kernel(
    sections, n_frame, n_row,
    counts, latents, cotangent, embed, kernel, tkernel, time_kernel, gain,
    spatial_out, temporal_out, sums_out,
    x_in, skip_in, x_out, u_in, u_skip, u_out, pad_x, pad_a, pad_u, pad_h, wide_x, wide_h,
    x_turned, a_turned, normed, grads, stat_src, slots, mask, width_mask, groups, bias,
    send_sem, recv_sem, *reduction,
):
    seg = lax.axis_index("segment")
    frame = lax.axis_index("frame")
    row = lax.axis_index("row")
    peers = n_frame * n_row
    me = frame * n_row + row
    last = sections - 1
    pending = []

    def member(index):
        return (seg, index // n_row, index % n_row)

    def remote(source, target, sem, device):
        return pltpu.make_async_remote_copy(
            src_ref=source,
            dst_ref=target,
            send_sem=send_sem.at[sem],
            recv_sem=recv_sem.at[sem],
            device_id=device,
            device_id_type=MESH,
        )

    def start_if(condition, copy):
        @pl.when(condition)
        def _():
            copy.start()

        pending.append((condition, copy))

    place = lax.broadcasted_iota(jnp.int32, (R_DEV * F_DEV, PAD, 1), 0) % F_DEV + frame * F_DEV
    column = lax.broadcasted_iota(jnp.int32, (R_DEV * F_DEV, PAD, 1), 1)
    for clip in range(CLIPS):
        live = (place < counts[clip]) & (column < WIDTH)
        mask[:, clip] = jnp.where(live, 1.0, 0.0)
    column = lax.broadcasted_iota(jnp.int32, (CELLS // PAD, PAD, 1), 1)
    width_mask[...] = jnp.where(column < WIDTH, 1.0, 0.0).reshape(CELLS, 1)
    ids = [lax.broadcasted_iota(jnp.int32, (C, C), dim).astype(jnp.float32) for dim in range(2)]
    ids = [jnp.floor((one + 0.5) * (G / C)) for one in ids]
    groups[...] = jnp.where(ids[0] == ids[1], 1.0, 0.0)
    bias[...] = dot_nn(embed[...], time_kernel[...])
    line = lax.broadcasted_iota(jnp.int32, (8, C), 0)
    in_use = jnp.where(line < 2, counts[0], counts[1]).astype(jnp.float32)
    inv_total = 1.0 / (in_use * (R_DEV * n_row * WIDTH * (C // G)))

    barrier = pltpu.get_barrier_semaphore()

    def greet(device):
        pl.semaphore_signal(barrier, inc=1, device_id=device, device_id_type=MESH)

    for step in range(1, peers):
        greet(member((me + step) % peers))

    @pl.when(seg > 0)
    def _():
        greet((seg - 1, frame, row))

    @pl.when(seg < last)
    def _():
        greet((seg + 1, frame, row))

    @pl.when((seg == 0) | (seg == last))
    def _():
        greet((last - seg, frame, row))

    linked = (seg > 0).astype(jnp.int32) + (seg < last).astype(jnp.int32)
    linked = linked + ((seg == 0) | (seg == last)).astype(jnp.int32)
    pl.semaphore_wait(barrier, peers - 1 + linked)

    after = (jnp.minimum(seg + 1, last), frame, row)
    before = (jnp.maximum(seg - 1, 0), frame, row)
    far = (last - seg, frame, row)
    x_copy = remote(x_out, x_in, 0, after)
    skip_copy = remote(x_out, skip_in, 1, far)
    u_copy = remote(u_out, u_in, 10, before)
    u_skip_copy = remote(u_out, u_skip, 11, far)

    def halo_start(padded, sem, index, size, at):
        onward = remote(
            padded.at[pl.ds(2 * BLOCK, BLOCK)], padded.at[pl.ds(0, BLOCK)],
            sem, at(jnp.minimum(index + 1, size - 1)),
        )
        back = remote(
            padded.at[pl.ds(BLOCK, BLOCK)], padded.at[pl.ds(3 * BLOCK, BLOCK)],
            sem + 1, at(jnp.maximum(index - 1, 0)),
        )
        start_if(index < size - 1, onward)
        start_if(index > 0, back)

        @pl.when(index == 0)
        def _():
            padded[pl.ds(0, BLOCK), :] = jnp.zeros((BLOCK, C), jnp.bfloat16)

        @pl.when(index == size - 1)
        def _():
            padded[pl.ds(3 * BLOCK, BLOCK), :] = jnp.zeros((BLOCK, C), jnp.bfloat16)

        return onward, back, index, size

    def halo_wait(started):
        onward, back, index, size = started

        @pl.when(index > 0)
        def _():
            onward.wait_recv()

        @pl.when(index < size - 1)
        def _():
            back.wait_recv()

    def row_start(padded, sem):
        return halo_start(padded, sem, row, n_row, lambda index: (seg, frame, index))

    def frame_start(padded, sem):
        return halo_start(padded, sem, frame, n_frame, lambda index: (seg, index, row))

    def exchange_start(turn, rows):
        stat_src[turn] = jnp.concatenate(rows + [jnp.zeros((8 - len(rows), C), jnp.float32)], axis=0)
        copies = []
        for step in range(1, peers):
            copy = remote(
                stat_src.at[turn], slots.at[turn, step - 1],
                12 + turn * (peers - 1) + step - 1, member((me + step) % peers),
            )
            copy.start()
            pending.append((None, copy))
            copies.append(copy)
        return turn, copies

    def exchange_wait(started):
        turn, copies = started
        total = stat_src[turn]
        for step, copy in enumerate(copies):
            copy.wait_recv()
            total = total + slots[turn, step]
        return total

    def column_sum(values):
        return jnp.sum(values.reshape(-1, C), axis=0, keepdims=True)

    def grouped(total):
        return lax.dot_general(
            total * inv_total, groups[...], (((1,), (0,)), ((), ())),
            precision=lax.Precision.HIGHEST, preferred_element_type=jnp.float32,
        )

    fused = bool(reduction)
    temporal_sum, spatial_sum = reduction[:2] if fused else (temporal_out, spatial_out)
    first_sem = 12 + 3 * (peers - 1)

    def stage(total, buffers):
        staged = buffers[0]
        rows = total.shape[0] // peers
        for index in range(peers):
            staged[index, :rows] = total[pl.ds(index * rows, rows), :].astype(jnp.bfloat16)
            if rows < staged.shape[1]:
                rest = staged.shape[1] - rows
                staged[index, rows:] = jnp.zeros((rest, C), jnp.bfloat16)

    def pair_start(buffers, turn):
        staged, landed = buffers[:2]
        other = 1 - frame
        copy = remote(
            staged.at[pl.ds(other * n_row, n_row)], landed,
            first_sem + turn * n_row, (seg, other, row),
        )
        copy.start()
        pending.append((None, copy))
        return copy

    def line_start(buffers, turn, pair):
        staged, landed, added, arrived = buffers
        pair.wait_recv()
        copies = []
        for step in range(n_row - 1, 0, -1):
            target = (row + step) % n_row
            mine = staged[frame * n_row + target].astype(jnp.float32)
            added[target] = (mine + landed[target].astype(jnp.float32)).astype(jnp.bfloat16)
            copy = remote(
                added.at[target], arrived.at[step - 1],
                first_sem + turn * n_row + step, (seg, frame, target),
            )
            copy.start()
            pending.append((None, copy))
            copies.append((step, copy))
        return copies

    def line_finish(buffers, copies, result):
        staged, landed, added, arrived = buffers
        total = staged[frame * n_row + row].astype(jnp.float32) + landed[row].astype(jnp.float32)
        for step, copy in copies:
            copy.wait_recv()
            total = total + arrived[step - 1].astype(jnp.float32)
        result[...] = total[: result.shape[0]]

    def spatial_pass(padded, wide, sem, term):
        halo = row_start(padded, sem)
        widen(padded, wide, BLOCK, CELLS)
        total = term(1, 0) + term(1, 1) + term(1, 2)
        halo_wait(halo)
        widen(padded, wide, 0, BLOCK)
        widen(padded, wide, 3 * BLOCK, BLOCK)
        for a in (0, 2):
            for b in range(3):
                total = total + term(a, b)
        return total

    def temporal_pass(padded, sem, term):
        halo = frame_start(padded, sem)
        total = term(1)
        halo_wait(halo)
        return total + term(0) + term(2)

    def turn():
        for b in range(3):
            x_turned[b] = jnp.transpose(wide_x[b], (1, 0))
        a_turned[...] = jnp.transpose(pad_a[...], (1, 0))

    def temporal_grad():
        for k in range(3):
            temporal_sum[pl.ds(k * C, C), :] = dot_nn(
                a_turned[:, pl.ds(k * BLOCK, CELLS)], pad_u[own, :]
            )
        if fused:
            stage(temporal_sum, reduction[2:6])

    own = pl.ds(BLOCK, CELLS)

    @pl.when(seg == 0)
    def _():
        pad_x[own, :] = jnp.zeros((CELLS, C), jnp.bfloat16)
        for r in range(R_DEV):
            for f in range(F_DEV):
                for clip in range(CLIPS):
                    start = BLOCK + ((r * F_DEV + f) * CLIPS + clip) * PAD
                    pad_x[pl.ds(start, WIDTH), :] = latents[clip, f, r]

    @pl.when(seg > 0)
    def _():
        x_copy.wait_recv()

    @pl.when((seg > 0) & (seg < last))
    def _():
        pad_x[own, :] = x_in[...]

    @pl.when(seg == last)
    def _():
        skip_copy.wait_recv()
        joined = x_in[...].astype(jnp.float32) + skip_in[...].astype(jnp.float32)
        pad_x[own, :] = joined.astype(jnp.bfloat16)

    hidden = spatial_pass(
        pad_x, wide_x, 2,
        lambda a, b: dot_nn(wide_x[b, pl.ds(a * BLOCK, CELLS), :], kernel[3 * a + b]),
    )
    normed[...] = hidden.reshape(normed.shape)
    rows = []
    for clip in range(CLIPS):
        part = normed[:, clip] + bias[pl.ds(clip, 1), :].reshape(1, 1, C)
        normed[:, clip] = part
        masked = part * mask[:, clip]
        rows += [column_sum(masked), column_sum(masked * part)]
    stats = exchange_start(0, rows)
    stats = grouped(exchange_wait(stats))
    inverses = []
    for clip in range(CLIPS):
        mean = stats[2 * clip : 2 * clip + 1]
        variance = stats[2 * clip + 1 : 2 * clip + 2] - mean * mean
        inverse = lax.rsqrt(variance + EPSILON)
        inverses.append(inverse)
        part = (normed[:, clip] - mean.reshape(1, 1, C)) * inverse.reshape(1, 1, C)
        normed[:, clip] = part
        scaled = part * gain[...].reshape(1, 1, C)
        grads[:, clip] = mask[:, clip] * (scaled * jax.nn.sigmoid(scaled))
    pad_a[own, :] = swap_order(grads[...].reshape(CELLS, C)).astype(jnp.bfloat16)
    temporal = temporal_pass(
        pad_a, 4, lambda k: dot_nn(pad_a[pl.ds(k * BLOCK, CELLS), :], tkernel[k])
    )

    @pl.when(seg < last)
    def _():
        x_out[...] = (pad_x[own, :].astype(jnp.float32) + swap_order(temporal)).astype(jnp.bfloat16)

    start_if(seg < last, x_copy)
    start_if(seg == 0, skip_copy)
    pl.when(seg < last)(turn)

    @pl.when(seg == last)
    def _():
        pad_u[own, :] = jnp.zeros((CELLS, C), jnp.bfloat16)
        for r in range(R_DEV):
            for f in range(F_DEV):
                for clip in range(CLIPS):
                    start = BLOCK + ((f * R_DEV + r) * CLIPS + clip) * PAD
                    kept = mask[r * F_DEV + f, clip][:WIDTH]
                    value = kept * cotangent[clip, f, r].astype(jnp.float32)
                    pad_u[pl.ds(start, WIDTH), :] = value.astype(jnp.bfloat16)

    @pl.when(seg < last)
    def _():
        u_copy.wait_recv()

    @pl.when((seg > 0) & (seg < last))
    def _():
        pad_u[own, :] = swap_order(u_in[...])

    @pl.when(seg == 0)
    def _():
        u_skip_copy.wait_recv()
        joined = u_in[...].astype(jnp.float32) + u_skip[...].astype(jnp.float32)
        pad_u[own, :] = swap_order(joined.astype(jnp.bfloat16))

    act_grad = temporal_pass(
        pad_u, 6, lambda k: dot_nt(pad_u[pl.ds(k * BLOCK, CELLS), :], tkernel[2 - k])
    )
    grads[...] = swap_order(act_grad).reshape(grads.shape)
    rows = []
    gain_part = jnp.zeros((1, C), jnp.float32)
    for clip in range(CLIPS):
        part = normed[:, clip]
        scaled = part * gain[...].reshape(1, 1, C)
        gate = jax.nn.sigmoid(scaled)
        scaled_grad = grads[:, clip] * mask[:, clip] * gate * (1.0 + scaled * (1.0 - gate))
        gain_part = gain_part + column_sum(scaled_grad * part)
        normed_grad = scaled_grad * gain[...].reshape(1, 1, C)
        grads[:, clip] = normed_grad
        rows += [column_sum(normed_grad), column_sum(normed_grad * part)]
    moments = exchange_start(1, rows)
    pl.when(seg == 0)(temporal_grad)
    moments = grouped(exchange_wait(moments))
    rows = []
    for clip in range(CLIPS):
        first = moments[2 * clip : 2 * clip + 1].reshape(1, 1, C)
        second = moments[2 * clip + 1 : 2 * clip + 2].reshape(1, 1, C)
        part = inverses[clip].reshape(1, 1, C) * (
            grads[:, clip] - mask[:, clip] * (first + normed[:, clip] * second)
        )
        part = part.astype(jnp.bfloat16).astype(jnp.float32)
        grads[:, clip] = part
        rows.append(column_sum(part))
    pad_h[own, :] = grads[...].reshape(CELLS, C).astype(jnp.bfloat16)
    @pl.when(seg > 0)
    def _():
        pending_before = len(pending)
        back = spatial_pass(
            pad_h, wide_h, 8,
            lambda a, b: dot_nt(wide_h[b, pl.ds(a * BLOCK, CELLS), :], kernel[8 - 3 * a - b]),
        )
        upstream = swap_order(pad_u[own, :]).astype(jnp.float32)
        u_out[...] = (upstream + back * width_mask[...]).astype(jnp.bfloat16)
        u_copy.start()
        for condition, copy in pending[pending_before:]:
            pl.when(condition)(copy.wait_send)
        del pending[pending_before:]

    @pl.when(seg == last)
    def _():
        u_skip_copy.start()
        turn()

    pl.when(seg > 0)(temporal_grad)
    sums = exchange_start(2, rows + [gain_part])
    if fused:
        temporal_pair = pair_start(reduction[2:6], 0)
    for a in range(3):
        if fused and a == 1:
            temporal_line = line_start(reduction[2:6], 0, temporal_pair)
        for b in range(3):
            spatial_sum[pl.ds((3 * a + b) * C, C), :] = dot_nn(
                x_turned[b, :, pl.ds(a * BLOCK, CELLS)], pad_h[own, :]
            )
    if fused:
        stage(spatial_sum, reduction[6:10])
        spatial_line = line_start(reduction[6:10], 1, pair_start(reduction[6:10], 1))
        line_finish(reduction[2:6], temporal_line, temporal_out)
        line_finish(reduction[6:10], spatial_line, spatial_out)
    sums_out[...] = exchange_wait(sums)
    for condition, copy in pending + [(seg > 0, u_copy), (seg == last, u_skip_copy)]:
        if condition is None:
            copy.wait_send()
        else:
            pl.when(condition)(copy.wait_send)


def run_section(sections, n_frame, n_row, *operands):
    peers = n_frame * n_row
    fused = n_frame == 2 and C * 3 % (8 * peers) == 0
    flat = pltpu.VMEM((CELLS, C), jnp.bfloat16)
    padded = pltpu.VMEM((2 * CELLS, C), jnp.bfloat16)
    field = pltpu.VMEM((R_DEV * F_DEV, CLIPS, PAD, C), jnp.float32)
    sems = 12 + 3 * (peers - 1) + 2 * n_row
    vmem = pl.BlockSpec(memory_space=pltpu.VMEM)
    smem = pl.BlockSpec(memory_space=pltpu.SMEM)
    taps = (3, 9)
    share = peers if fused else 1
    reduction = []
    if fused:
        reduction = [pltpu.VMEM((count * C, C), jnp.float32) for count in taps]
        for count in taps:
            rows = -(-count * C // (16 * peers)) * 16
            reduction += [
                pltpu.VMEM((held, rows, C), jnp.bfloat16) for held in (peers, n_row, n_row, n_row - 1)
            ]
    return pl.pallas_call(
        functools.partial(section_kernel, sections, n_frame, n_row),
        out_shape=(
            jax.ShapeDtypeStruct((9 * C // share, C), jnp.float32),
            jax.ShapeDtypeStruct((3 * C // share, C), jnp.float32),
            jax.ShapeDtypeStruct((8, C), jnp.float32),
        ),
        in_specs=[smem] + [vmem] * (len(operands) - 1),
        out_specs=(vmem, vmem, vmem),
        scratch_shapes=[flat] * 6
        + [padded] * 4
        + [pltpu.VMEM((3, 2 * CELLS, C), jnp.bfloat16)] * 2
        + [
            pltpu.VMEM((3, C, 2 * CELLS), jnp.bfloat16),
            pltpu.VMEM((C, 2 * CELLS), jnp.bfloat16),
            field,
            field,
            pltpu.VMEM((3, 8, C), jnp.float32),
            pltpu.VMEM((3, peers - 1, 8, C), jnp.float32),
            pltpu.VMEM((R_DEV * F_DEV, CLIPS, PAD, 1), jnp.float32),
            pltpu.VMEM((CELLS, 1), jnp.float32),
            pltpu.VMEM((C, C), jnp.float32),
            pltpu.VMEM((16, C), jnp.float32),
            pltpu.SemaphoreType.DMA((sems,)),
            pltpu.SemaphoreType.DMA((sems,)),
        ]
        + reduction,
        compiler_params=pltpu.CompilerParams(
            collective_id=0, has_side_effects=True, vmem_limit_bytes=56 * 1024 * 1024
        ),
    )(*operands)


def per_device(
    latents,
    cotangent,
    timesteps,
    frame_counts,
    spatial_weight,
    temporal_weight,
    time_weight,
    norm_gain,
):
    sections = lax.axis_size("segment")
    n_frame = lax.axis_size("frame")
    n_row = lax.axis_size("row")
    peers = n_frame * n_row
    me = lax.axis_index("frame") * n_row + lax.axis_index("row")
    time_embed = time_features(jnp.pad(timesteps, (0, 16 - CLIPS)))
    spatial, temporal, sums = run_section(
        sections,
        n_frame,
        n_row,
        frame_counts,
        latents,
        cotangent,
        time_embed,
        spatial_weight[0],
        temporal_weight[0],
        time_weight[0],
        norm_gain,
    )
    if spatial.shape[0] == 9 * C:
        parts = [spatial.reshape(peers, -1, C), temporal.reshape(peers, -1, C)]
        parts = jnp.concatenate(parts, axis=1).astype(jnp.bfloat16)
        reduced = lax.psum_scatter(parts, ("frame", "row"), scatter_dimension=0, tiled=True)[0]
        reduced = reduced.astype(jnp.float32)
        spatial, temporal = reduced[: 9 * C // peers], reduced[9 * C // peers :]
    time_rows = TE // peers
    embed = lax.dynamic_slice_in_dim(time_embed, me * time_rows, time_rows, 1).astype(jnp.float32)
    time_out = embed[0][:, None] * sums[0][None, :]
    for clip in range(1, CLIPS):
        time_out = time_out + embed[clip][:, None] * sums[clip][None, :]
    gain_out = lax.dynamic_slice_in_dim(sums[CLIPS], me * (C // peers), C // peers, 0)
    return (spatial[None], temporal[None], time_out[None], gain_out[None])


def solution(mesh):
    return jax.shard_map(
        per_device,
        mesh=mesh,
        in_specs=(
            P(None, "frame", "row", None, None),
            P(None, "frame", "row", None, None),
            P(),
            P(),
            P("segment", None, None, None),
            P("segment", None, None, None),
            P("segment", None, None),
            P("segment", None),
        ),
        out_specs=(
            P("segment", ("frame", "row"), None),
            P("segment", ("frame", "row"), None),
            P("segment", ("frame", "row"), None),
            P("segment", ("frame", "row")),
        ),
        check_vma=False,
    )
```

```python
import functools

import jax
import jax.numpy as jnp
from jax import lax
from jax.experimental import pallas as pl
from jax.experimental.pallas import tpu as pltpu
from jax.sharding import PartitionSpec as P

C = 320
G = 32
TE = 1280
WIDTH = 24
R_DEV = 2
F_DEV = 2
CLIPS = 2


EPSILON = 1e-05


def time_features(timesteps):
    half_dim = TE // 2
    frequency = jnp.exp(-jnp.log(10000.0) * jnp.arange(half_dim).astype(jnp.float32) / half_dim)
    angles = timesteps.astype(jnp.float32)[:, None] * frequency[None, :]
    wave_parts = jnp.concatenate([jnp.cos(angles), jnp.sin(angles)], axis=1)
    return jax.nn.silu(wave_parts).astype(jnp.bfloat16)


PAD = 32
BLOCK = F_DEV * PAD
CELLS = R_DEV * BLOCK
LINKS = 12
TURNS = 2 * CLIPS + 1
MESH = pl.DeviceIdType.MESH


def swap_order(flat):
    return jnp.concatenate(
        [flat[:PAD], flat[2 * PAD : 3 * PAD], flat[PAD : 2 * PAD], flat[3 * PAD :]], axis=0
    )


def dot_nn(left, right):
    return lax.dot_general(left, right, (((1,), (0,)), ((), ())), preferred_element_type=jnp.float32)


def dot_nt(left, right):
    return lax.dot_general(left, right, (((1,), (1,)), ((), ())), preferred_element_type=jnp.float32)


def widen(padded, wide, start, length):
    some = pl.ds(start, length)
    values = padded[some, :]
    exact = values.astype(jnp.float32)
    wide[0, some, :] = pltpu.roll(exact, 1, 0).astype(jnp.bfloat16)
    wide[1, some, :] = values
    wide[2, some, :] = pltpu.roll(exact, length - 1, 0).astype(jnp.bfloat16)


def section_kernel(
    sections, n_frame, n_row,
    counts, latents, cotangent, embed, kernel, tkernel, time_kernel, gain,
    spatial_out, temporal_out, sums_out,
    x_in, skip_in, x_out, u_in, u_skip, u_out, pad_x, pad_a, pad_u, pad_h, wide_x, wide_h,
    x_turned, a_turned, normed, grads, stat_src, slots, mask, width_mask, groups, bias,
    send_sem, recv_sem, *reduction,
):
    seg = lax.axis_index("segment")
    frame = lax.axis_index("frame")
    row = lax.axis_index("row")
    peers = n_frame * n_row
    me = frame * n_row + row
    last = sections - 1
    pending = []

    def member(index):
        return (seg, index // n_row, index % n_row)

    def remote(source, target, sem, device):
        return pltpu.make_async_remote_copy(
            src_ref=source,
            dst_ref=target,
            send_sem=send_sem.at[sem],
            recv_sem=recv_sem.at[sem],
            device_id=device,
            device_id_type=MESH,
        )

    def start_if(condition, copy):
        @pl.when(condition)
        def _():
            copy.start()

        pending.append((condition, copy))

    place = lax.broadcasted_iota(jnp.int32, (R_DEV * F_DEV, PAD, 1), 0) % F_DEV + frame * F_DEV
    column = lax.broadcasted_iota(jnp.int32, (R_DEV * F_DEV, PAD, 1), 1)
    for clip in range(CLIPS):
        live = (place < counts[clip]) & (column < WIDTH)
        mask[clip] = jnp.where(live, 1.0, 0.0)
    column = lax.broadcasted_iota(jnp.int32, (CELLS // PAD, PAD, 1), 1)
    width_mask[...] = jnp.where(column < WIDTH, 1.0, 0.0).reshape(CELLS, 1)
    ids = [lax.broadcasted_iota(jnp.int32, (C, C), dim).astype(jnp.float32) for dim in range(2)]
    ids = [jnp.floor((one + 0.5) * (G / C)) for one in ids]
    groups[...] = jnp.where(ids[0] == ids[1], 1.0, 0.0)
    bias[...] = dot_nn(embed[...], time_kernel[...])
    inv_totals = []
    for clip in range(CLIPS):
        in_use = jnp.full((8, C), counts[clip], jnp.int32).astype(jnp.float32)
        inv_totals.append(1.0 / (in_use * (R_DEV * n_row * WIDTH * (C // G))))

    barrier = pltpu.get_barrier_semaphore()

    def greet(device):
        pl.semaphore_signal(barrier, inc=1, device_id=device, device_id_type=MESH)

    for step in range(1, peers):
        greet(member((me + step) % peers))

    @pl.when(seg > 0)
    def _():
        greet((seg - 1, frame, row))

    @pl.when(seg < last)
    def _():
        greet((seg + 1, frame, row))

    @pl.when((seg == 0) | (seg == last))
    def _():
        greet((last - seg, frame, row))

    linked = (seg > 0).astype(jnp.int32) + (seg < last).astype(jnp.int32)
    linked = linked + ((seg == 0) | (seg == last)).astype(jnp.int32)
    pl.semaphore_wait(barrier, peers - 1 + linked)

    after = (jnp.minimum(seg + 1, last), frame, row)
    before = (jnp.maximum(seg - 1, 0), frame, row)
    far = (last - seg, frame, row)

    def hops(source, target, sem, device):
        return [
            remote(source.at[clip], target.at[clip], sem + LINKS * clip, device)
            for clip in range(CLIPS)
        ]

    x_copy = hops(x_out, x_in, 0, after)
    skip_copy = hops(x_out, skip_in, 1, far)
    u_copy = hops(u_out, u_in, 10, before)
    u_skip_copy = hops(u_out, u_skip, 11, far)

    def halo_start(padded, sem, index, size, at):
        onward = remote(
            padded.at[pl.ds(2 * BLOCK, BLOCK)], padded.at[pl.ds(0, BLOCK)],
            sem, at(jnp.minimum(index + 1, size - 1)),
        )
        back = remote(
            padded.at[pl.ds(BLOCK, BLOCK)], padded.at[pl.ds(3 * BLOCK, BLOCK)],
            sem + 1, at(jnp.maximum(index - 1, 0)),
        )
        start_if(index < size - 1, onward)
        start_if(index > 0, back)

        @pl.when(index == 0)
        def _():
            padded[pl.ds(0, BLOCK), :] = jnp.zeros((BLOCK, C), jnp.bfloat16)

        @pl.when(index == size - 1)
        def _():
            padded[pl.ds(3 * BLOCK, BLOCK), :] = jnp.zeros((BLOCK, C), jnp.bfloat16)

        return onward, back, index, size

    def halo_wait(started):
        onward, back, index, size = started

        @pl.when(index > 0)
        def _():
            onward.wait_recv()

        @pl.when(index < size - 1)
        def _():
            back.wait_recv()

    def row_start(padded, sem):
        return halo_start(padded, sem, row, n_row, lambda index: (seg, frame, index))

    def frame_start(padded, sem):
        return halo_start(padded, sem, frame, n_frame, lambda index: (seg, index, row))

    def exchange_start(turn, rows):
        stat_src[turn] = jnp.concatenate(rows + [jnp.zeros((8 - len(rows), C), jnp.float32)], axis=0)
        copies = []
        for step in range(1, peers):
            copy = remote(
                stat_src.at[turn], slots.at[turn, step - 1],
                LINKS * CLIPS + turn * (peers - 1) + step - 1, member((me + step) % peers),
            )
            copy.start()
            pending.append((None, copy))
            copies.append(copy)
        return turn, copies

    def exchange_wait(started):
        turn, copies = started
        total = stat_src[turn]
        for step, copy in enumerate(copies):
            copy.wait_recv()
            total = total + slots[turn, step]
        return total

    def column_sum(values):
        return jnp.sum(values.reshape(-1, C), axis=0, keepdims=True)

    def grouped(total, inv_total):
        return lax.dot_general(
            total * inv_total, groups[...], (((1,), (0,)), ((), ())),
            precision=lax.Precision.HIGHEST, preferred_element_type=jnp.float32,
        )

    fused = bool(reduction)
    temporal_sum, spatial_sum = reduction[:2] if fused else (temporal_out, spatial_out)
    first_sem = LINKS * CLIPS + TURNS * (peers - 1)

    def stage(total, buffers):
        staged = buffers[0]
        rows = total.shape[0] // peers
        for index in range(peers):
            staged[index, :rows] = total[pl.ds(index * rows, rows), :].astype(jnp.bfloat16)
            if rows < staged.shape[1]:
                rest = staged.shape[1] - rows
                staged[index, rows:] = jnp.zeros((rest, C), jnp.bfloat16)

    def pair_start(buffers, turn):
        staged, landed = buffers[:2]
        other = 1 - frame
        copy = remote(
            staged.at[pl.ds(other * n_row, n_row)], landed,
            first_sem + turn * n_row, (seg, other, row),
        )
        copy.start()
        pending.append((None, copy))
        return copy

    def line_start(buffers, turn, pair):
        staged, landed, added, arrived = buffers
        pair.wait_recv()
        copies = []
        for step in range(n_row - 1, 0, -1):
            target = (row + step) % n_row
            mine = staged[frame * n_row + target].astype(jnp.float32)
            added[target] = (mine + landed[target].astype(jnp.float32)).astype(jnp.bfloat16)
            copy = remote(
                added.at[target], arrived.at[step - 1],
                first_sem + turn * n_row + step, (seg, frame, target),
            )
            copy.start()
            pending.append((None, copy))
            copies.append((step, copy))
        return copies

    def line_finish(buffers, copies, result):
        staged, landed, added, arrived = buffers
        total = staged[frame * n_row + row].astype(jnp.float32) + landed[row].astype(jnp.float32)
        for step, copy in copies:
            copy.wait_recv()
            total = total + arrived[step - 1].astype(jnp.float32)
        result[...] = total[: result.shape[0]]

    def spatial_pass(padded, wide, halo, term):
        widen(padded, wide, BLOCK, CELLS)
        total = term(1, 0) + term(1, 1) + term(1, 2)
        halo_wait(halo)
        widen(padded, wide, 0, BLOCK)
        widen(padded, wide, 3 * BLOCK, BLOCK)
        for a in (0, 2):
            for b in range(3):
                total = total + term(a, b)
        return total

    def temporal_pass(halo, term):
        total = term(1)
        halo_wait(halo)
        return total + term(0) + term(2)

    def both(padded):
        return jnp.concatenate([padded[clip, own, :] for clip in range(CLIPS)], axis=0)

    def turn():
        for clip in range(CLIPS):
            part = pl.ds(clip * CELLS, CELLS)
            for a in range(3):
                for b in range(3):
                    rows = wide_x[clip, b, pl.ds(a * BLOCK, CELLS), :]
                    x_turned[3 * a + b, :, part] = jnp.transpose(rows, (1, 0))
                rows = pad_a[clip, pl.ds(a * BLOCK, CELLS), :]
                a_turned[a, :, part] = jnp.transpose(rows, (1, 0))

    def temporal_grad():
        upstream = both(pad_u)
        for k in range(3):
            temporal_sum[pl.ds(k * C, C), :] = dot_nn(a_turned[k], upstream)
        if fused:
            stage(temporal_sum, reduction[2:6])

    own = pl.ds(BLOCK, CELLS)
    stats = []
    for clip in range(CLIPS):

        @pl.when(seg == 0)
        def _():
            pad_x[clip, own, :] = jnp.zeros((CELLS, C), jnp.bfloat16)
            for r in range(R_DEV):
                for f in range(F_DEV):
                    start = BLOCK + (r * F_DEV + f) * PAD
                    pad_x[clip, pl.ds(start, WIDTH), :] = latents[clip, f, r]

        @pl.when(seg > 0)
        def _():
            x_copy[clip].wait_recv()

        @pl.when((seg > 0) & (seg < last))
        def _():
            pad_x[clip, own, :] = x_in[clip]

        @pl.when(seg == last)
        def _():
            skip_copy[clip].wait_recv()
            joined = x_in[clip].astype(jnp.float32) + skip_in[clip].astype(jnp.float32)
            pad_x[clip, own, :] = joined.astype(jnp.bfloat16)

        wide = wide_x.at[clip]
        hidden = spatial_pass(
            pad_x.at[clip], wide, row_start(pad_x.at[clip], 2 + LINKS * clip),
            lambda a, b: dot_nn(wide[b, pl.ds(a * BLOCK, CELLS), :], kernel[3 * a + b]),
        )
        hidden = hidden + bias[pl.ds(clip, 1), :]
        part = hidden.reshape(R_DEV * F_DEV, PAD, C)
        normed[clip] = part
        masked = part * mask[clip]
        stats.append(exchange_start(clip, [column_sum(masked), column_sum(masked * part)]))
    inverses = []
    halos = []
    for clip in range(CLIPS):
        group = grouped(exchange_wait(stats[clip]), inv_totals[clip])
        mean = group[0:1]
        inverse = lax.rsqrt(group[1:2] - mean * mean + EPSILON)
        inverses.append(inverse)
        part = (normed[clip] - mean.reshape(1, 1, C)) * inverse.reshape(1, 1, C)
        normed[clip] = part
        scaled = part * gain[...].reshape(1, 1, C)
        active = mask[clip] * (scaled * jax.nn.sigmoid(scaled))
        pad_a[clip, own, :] = swap_order(active.reshape(CELLS, C)).astype(jnp.bfloat16)
        halos.append(frame_start(pad_a.at[clip], 4 + LINKS * clip))
    for clip in range(CLIPS):
        temporal = temporal_pass(
            halos[clip], lambda k: dot_nn(pad_a[clip, pl.ds(k * BLOCK, CELLS), :], tkernel[k])
        )

        @pl.when(seg < last)
        def _():
            total = pad_x[clip, own, :].astype(jnp.float32) + swap_order(temporal)
            x_out[clip] = total.astype(jnp.bfloat16)

        start_if(seg < last, x_copy[clip])
        start_if(seg == 0, skip_copy[clip])
    pl.when(seg < last)(turn)

    gain_part = jnp.zeros((1, C), jnp.float32)
    moments = []
    for clip in range(CLIPS):

        @pl.when(seg == last)
        def _():
            pad_u[clip, own, :] = jnp.zeros((CELLS, C), jnp.bfloat16)
            for r in range(R_DEV):
                for f in range(F_DEV):
                    start = BLOCK + (f * R_DEV + r) * PAD
                    kept = mask[clip, r * F_DEV + f][:WIDTH]
                    value = kept * cotangent[clip, f, r].astype(jnp.float32)
                    pad_u[clip, pl.ds(start, WIDTH), :] = value.astype(jnp.bfloat16)

        @pl.when(seg < last)
        def _():
            u_copy[clip].wait_recv()

        @pl.when((seg > 0) & (seg < last))
        def _():
            pad_u[clip, own, :] = swap_order(u_in[clip])

        @pl.when(seg == 0)
        def _():
            u_skip_copy[clip].wait_recv()
            joined = u_in[clip].astype(jnp.float32) + u_skip[clip].astype(jnp.float32)
            pad_u[clip, own, :] = swap_order(joined.astype(jnp.bfloat16))

        act_grad = temporal_pass(
            frame_start(pad_u.at[clip], 6 + LINKS * clip),
            lambda k: dot_nt(pad_u[clip, pl.ds(k * BLOCK, CELLS), :], tkernel[2 - k]),
        )
        act_grad = swap_order(act_grad).reshape(R_DEV * F_DEV, PAD, C)
        part = normed[clip]
        scaled = part * gain[...].reshape(1, 1, C)
        gate = jax.nn.sigmoid(scaled)
        scaled_grad = act_grad * mask[clip] * gate * (1.0 + scaled * (1.0 - gate))
        normed_grad = scaled_grad * gain[...].reshape(1, 1, C)
        grads[clip] = normed_grad
        rows = [column_sum(normed_grad), column_sum(normed_grad * part)]
        moments.append(exchange_start(CLIPS + clip, rows))
        gain_part = gain_part + column_sum(scaled_grad * part)
    pl.when(seg == 0)(temporal_grad)
    rows = []
    for clip in range(CLIPS):
        group = grouped(exchange_wait(moments[clip]), inv_totals[clip])
        first, second = group[0:1].reshape(1, 1, C), group[1:2].reshape(1, 1, C)
        part = inverses[clip].reshape(1, 1, C) * (
            grads[clip] - mask[clip] * (first + normed[clip] * second)
        )
        part = part.astype(jnp.bfloat16)
        pad_h[clip, own, :] = part.reshape(CELLS, C)
        rows.append(column_sum(part.astype(jnp.float32)))

    @pl.when(seg > 0)
    def _():
        pending_before = len(pending)
        halos = [row_start(pad_h.at[clip], 8 + LINKS * clip) for clip in range(CLIPS)]
        for clip in range(CLIPS):
            wide = wide_h.at[clip]
            back = spatial_pass(
                pad_h.at[clip], wide, halos[clip],
                lambda a, b: dot_nt(wide[b, pl.ds(a * BLOCK, CELLS), :], kernel[8 - 3 * a - b]),
            )
            upstream = swap_order(pad_u[clip, own, :]).astype(jnp.float32)
            u_out[clip] = (upstream + back * width_mask[...]).astype(jnp.bfloat16)
            u_copy[clip].start()
            pl.when(seg == last)(u_skip_copy[clip].start)
        for condition, copy in pending[pending_before:]:
            pl.when(condition)(copy.wait_send)
        del pending[pending_before:]

    pl.when(seg == last)(turn)
    pl.when(seg > 0)(temporal_grad)
    sums = exchange_start(2 * CLIPS, rows + [gain_part])
    if fused:
        temporal_pair = pair_start(reduction[2:6], 0)
    hidden_grad = both(pad_h)
    for a in range(3):
        if fused and a == 1:
            temporal_line = line_start(reduction[2:6], 0, temporal_pair)
        for b in range(3):
            spatial_sum[pl.ds((3 * a + b) * C, C), :] = dot_nn(x_turned[3 * a + b], hidden_grad)
    if fused:
        stage(spatial_sum, reduction[6:10])
        spatial_line = line_start(reduction[6:10], 1, pair_start(reduction[6:10], 1))
        line_finish(reduction[2:6], temporal_line, temporal_out)
        line_finish(reduction[6:10], spatial_line, spatial_out)
    sums_out[...] = exchange_wait(sums)
    pending += [(seg > 0, copy) for copy in u_copy] + [(seg == last, copy) for copy in u_skip_copy]
    for condition, copy in pending:
        if condition is None:
            copy.wait_send()
        else:
            pl.when(condition)(copy.wait_send)


def run_section(sections, n_frame, n_row, *operands):
    peers = n_frame * n_row
    fused = n_frame == 2 and C * 3 % (8 * peers) == 0
    flat = pltpu.VMEM((CLIPS, CELLS, C), jnp.bfloat16)
    padded = pltpu.VMEM((CLIPS, 2 * CELLS, C), jnp.bfloat16)
    field = pltpu.VMEM((CLIPS, R_DEV * F_DEV, PAD, C), jnp.float32)
    sems = LINKS * CLIPS + TURNS * (peers - 1) + 2 * n_row
    vmem = pl.BlockSpec(memory_space=pltpu.VMEM)
    smem = pl.BlockSpec(memory_space=pltpu.SMEM)
    taps = (3, 9)
    share = peers if fused else 1
    reduction = []
    if fused:
        reduction = [pltpu.VMEM((count * C, C), jnp.float32) for count in taps]
        for count in taps:
            rows = -(-count * C // (16 * peers)) * 16
            reduction += [
                pltpu.VMEM((held, rows, C), jnp.bfloat16) for held in (peers, n_row, n_row, n_row - 1)
            ]
    return pl.pallas_call(
        functools.partial(section_kernel, sections, n_frame, n_row),
        out_shape=(
            jax.ShapeDtypeStruct((9 * C // share, C), jnp.float32),
            jax.ShapeDtypeStruct((3 * C // share, C), jnp.float32),
            jax.ShapeDtypeStruct((8, C), jnp.float32),
        ),
        in_specs=[smem] + [vmem] * (len(operands) - 1),
        out_specs=(vmem, vmem, vmem),
        scratch_shapes=[flat] * 6
        + [padded] * 4
        + [pltpu.VMEM((CLIPS, 3, 2 * CELLS, C), jnp.bfloat16)] * 2
        + [
            pltpu.VMEM((9, C, CLIPS * CELLS), jnp.bfloat16),
            pltpu.VMEM((3, C, CLIPS * CELLS), jnp.bfloat16),
            field,
            field,
            pltpu.VMEM((TURNS, 8, C), jnp.float32),
            pltpu.VMEM((TURNS, peers - 1, 8, C), jnp.float32),
            pltpu.VMEM((CLIPS, R_DEV * F_DEV, PAD, 1), jnp.float32),
            pltpu.VMEM((CELLS, 1), jnp.float32),
            pltpu.VMEM((C, C), jnp.float32),
            pltpu.VMEM((16, C), jnp.float32),
            pltpu.SemaphoreType.DMA((sems,)),
            pltpu.SemaphoreType.DMA((sems,)),
        ]
        + reduction,
        compiler_params=pltpu.CompilerParams(
            collective_id=0, has_side_effects=True, vmem_limit_bytes=56 * 1024 * 1024
        ),
    )(*operands)


def per_device(
    latents,
    cotangent,
    timesteps,
    frame_counts,
    spatial_weight,
    temporal_weight,
    time_weight,
    norm_gain,
):
    sections = lax.axis_size("segment")
    n_frame = lax.axis_size("frame")
    n_row = lax.axis_size("row")
    peers = n_frame * n_row
    me = lax.axis_index("frame") * n_row + lax.axis_index("row")
    time_embed = time_features(jnp.pad(timesteps, (0, 16 - CLIPS)))
    spatial, temporal, sums = run_section(
        sections,
        n_frame,
        n_row,
        frame_counts,
        latents,
        cotangent,
        time_embed,
        spatial_weight[0],
        temporal_weight[0],
        time_weight[0],
        norm_gain,
    )
    if spatial.shape[0] == 9 * C:
        parts = [spatial.reshape(peers, -1, C), temporal.reshape(peers, -1, C)]
        parts = jnp.concatenate(parts, axis=1).astype(jnp.bfloat16)
        reduced = lax.psum_scatter(parts, ("frame", "row"), scatter_dimension=0, tiled=True)[0]
        reduced = reduced.astype(jnp.float32)
        spatial, temporal = reduced[: 9 * C // peers], reduced[9 * C // peers :]
    time_rows = TE // peers
    embed = lax.dynamic_slice_in_dim(time_embed, me * time_rows, time_rows, 1).astype(jnp.float32)
    time_out = embed[0][:, None] * sums[0][None, :]
    for clip in range(1, CLIPS):
        time_out = time_out + embed[clip][:, None] * sums[clip][None, :]
    gain_out = lax.dynamic_slice_in_dim(sums[CLIPS], me * (C // peers), C // peers, 0)
    return (spatial[None], temporal[None], time_out[None], gain_out[None])


def solution(mesh):
    return jax.shard_map(
        per_device,
        mesh=mesh,
        in_specs=(
            P(None, "frame", "row", None, None),
            P(None, "frame", "row", None, None),
            P(),
            P(),
            P("segment", None, None, None),
            P("segment", None, None, None),
            P("segment", None, None),
            P("segment", None),
        ),
        out_specs=(
            P("segment", ("frame", "row"), None),
            P("segment", ("frame", "row"), None),
            P("segment", ("frame", "row"), None),
            P("segment", ("frame", "row")),
        ),
        check_vma=False,
    )
```

```python
import functools

import jax
import jax.numpy as jnp
from jax import lax
from jax.experimental import pallas as pl
from jax.experimental.pallas import tpu as pltpu
from jax.sharding import PartitionSpec as P

C = 320
G = 32
TE = 1280
WIDTH = 24
R_DEV = 2
F_DEV = 2
CLIPS = 2


EPSILON = 1e-05


def time_features(timesteps):
    half_dim = TE // 2
    frequency = jnp.exp(-jnp.log(10000.0) * jnp.arange(half_dim).astype(jnp.float32) / half_dim)
    angles = timesteps.astype(jnp.float32)[:, None] * frequency[None, :]
    wave_parts = jnp.concatenate([jnp.cos(angles), jnp.sin(angles)], axis=1)
    return jax.nn.silu(wave_parts).astype(jnp.bfloat16)


PAD = 32
BLOCK = F_DEV * CLIPS * PAD
CELLS = R_DEV * BLOCK
HALF = CLIPS * PAD
MESH = pl.DeviceIdType.MESH


def swap_order(flat):
    return jnp.concatenate(
        [flat[:HALF], flat[2 * HALF : 3 * HALF], flat[HALF : 2 * HALF], flat[3 * HALF :]], axis=0
    )


def dot_nn(left, right):
    return lax.dot_general(left, right, (((1,), (0,)), ((), ())), preferred_element_type=jnp.float32)


def widen(padded, wide, start, length):
    some = pl.ds(start, length)
    values = padded[some, :]
    exact = values.astype(jnp.float32)
    wide[some, :C] = pltpu.roll(exact, 1, 0).astype(jnp.bfloat16)
    wide[some, C : 2 * C] = values
    wide[some, 2 * C :] = pltpu.roll(exact, length - 1, 0).astype(jnp.bfloat16)


def section_kernel(
    sections, n_frame, n_row,
    counts, latents, cotangent, embed, kernel, tkernel, time_kernel, gain,
    spatial_out, temporal_out, sums_out,
    x_in, skip_in, x_out, u_in, u_skip, u_out, pad_x, pad_a, pad_u, pad_h, wide_x, wide_h,
    x_turned, a_turned, normed, grads, stat_src, slots, mask, width_mask, groups, bias, kernel_back, tkernel_back,
    send_sem, recv_sem, *reduction,
):
    seg = lax.axis_index("segment")
    frame = lax.axis_index("frame")
    row = lax.axis_index("row")
    peers = n_frame * n_row
    me = frame * n_row + row
    last = sections - 1
    pending = []

    def member(index):
        return (seg, index // n_row, index % n_row)

    def remote(source, target, sem, device):
        return pltpu.make_async_remote_copy(
            src_ref=source,
            dst_ref=target,
            send_sem=send_sem.at[sem],
            recv_sem=recv_sem.at[sem],
            device_id=device,
            device_id_type=MESH,
        )

    def start_if(condition, copy):
        @pl.when(condition)
        def _():
            copy.start()

        pending.append((condition, copy))

    place = lax.broadcasted_iota(jnp.int32, (R_DEV * F_DEV, PAD, 1), 0) % F_DEV + frame * F_DEV
    column = lax.broadcasted_iota(jnp.int32, (R_DEV * F_DEV, PAD, 1), 1)
    for clip in range(CLIPS):
        live = (place < counts[clip]) & (column < WIDTH)
        mask[:, clip] = jnp.where(live, 1.0, 0.0)
    column = lax.broadcasted_iota(jnp.int32, (CELLS // PAD, PAD, 1), 1)
    width_mask[...] = jnp.where(column < WIDTH, 1.0, 0.0).reshape(CELLS, 1)
    ids = [lax.broadcasted_iota(jnp.int32, (C, C), dim).astype(jnp.float32) for dim in range(2)]
    ids = [jnp.floor((one + 0.5) * (G / C)) for one in ids]
    groups[...] = jnp.where(ids[0] == ids[1], 1.0, 0.0)
    bias[...] = dot_nn(embed[...], time_kernel[...])
    line = lax.broadcasted_iota(jnp.int32, (8, C), 0)
    in_use = jnp.where(line < 2, counts[0], counts[1]).astype(jnp.float32)
    inv_total = 1.0 / (in_use * (R_DEV * n_row * WIDTH * (C // G)))

    barrier = pltpu.get_barrier_semaphore()

    def greet(device):
        pl.semaphore_signal(barrier, inc=1, device_id=device, device_id_type=MESH)

    for step in range(1, peers):
        greet(member((me + step) % peers))

    @pl.when(seg > 0)
    def _():
        greet((seg - 1, frame, row))

    @pl.when(seg < last)
    def _():
        greet((seg + 1, frame, row))

    @pl.when((seg == 0) | (seg == last))
    def _():
        greet((last - seg, frame, row))

    linked = (seg > 0).astype(jnp.int32) + (seg < last).astype(jnp.int32)
    linked = linked + ((seg == 0) | (seg == last)).astype(jnp.int32)
    pl.semaphore_wait(barrier, peers - 1 + linked)

    after = (jnp.minimum(seg + 1, last), frame, row)
    before = (jnp.maximum(seg - 1, 0), frame, row)
    far = (last - seg, frame, row)
    x_copy = remote(x_out, x_in, 0, after)
    skip_copy = remote(x_out, skip_in, 1, far)
    u_copy = remote(u_out, u_in, 10, before)
    u_skip_copy = remote(u_out, u_skip, 11, far)

    def halo_start(padded, sem, index, size, at):
        onward = remote(
            padded.at[pl.ds(2 * BLOCK, BLOCK)], padded.at[pl.ds(0, BLOCK)],
            sem, at(jnp.minimum(index + 1, size - 1)),
        )
        back = remote(
            padded.at[pl.ds(BLOCK, BLOCK)], padded.at[pl.ds(3 * BLOCK, BLOCK)],
            sem + 1, at(jnp.maximum(index - 1, 0)),
        )
        start_if(index < size - 1, onward)
        start_if(index > 0, back)

        @pl.when(index == 0)
        def _():
            padded[pl.ds(0, BLOCK), :] = jnp.zeros((BLOCK, C), jnp.bfloat16)

        @pl.when(index == size - 1)
        def _():
            padded[pl.ds(3 * BLOCK, BLOCK), :] = jnp.zeros((BLOCK, C), jnp.bfloat16)

        return onward, back, index, size

    def halo_wait(started):
        onward, back, index, size = started

        @pl.when(index > 0)
        def _():
            onward.wait_recv()

        @pl.when(index < size - 1)
        def _():
            back.wait_recv()

    def row_start(padded, sem):
        return halo_start(padded, sem, row, n_row, lambda index: (seg, frame, index))

    def frame_start(padded, sem):
        return halo_start(padded, sem, frame, n_frame, lambda index: (seg, index, row))

    def exchange_start(turn, rows):
        stat_src[turn] = jnp.concatenate(rows + [jnp.zeros((8 - len(rows), C), jnp.float32)], axis=0)
        copies = []
        for step in range(1, peers):
            copy = remote(
                stat_src.at[turn], slots.at[turn, step - 1],
                12 + turn * (peers - 1) + step - 1, member((me + step) % peers),
            )
            copy.start()
            pending.append((None, copy))
            copies.append(copy)
        return turn, copies

    def exchange_wait(started):
        turn, copies = started
        total = stat_src[turn]
        for step, copy in enumerate(copies):
            copy.wait_recv()
            total = total + slots[turn, step]
        return total

    def column_sum(values):
        return jnp.sum(values.reshape(-1, C), axis=0, keepdims=True)

    def grouped(total):
        return lax.dot_general(
            total * inv_total, groups[...], (((1,), (0,)), ((), ())),
            precision=lax.Precision.HIGHEST, preferred_element_type=jnp.float32,
        )

    fused = bool(reduction)
    temporal_sum, spatial_sum = reduction[:2] if fused else (temporal_out, spatial_out)
    first_sem = 12 + 3 * (peers - 1)

    def stage(total, buffers):
        staged = buffers[0]
        rows = total.shape[0] // peers
        for index in range(peers):
            staged[index, :rows] = total[pl.ds(index * rows, rows), :].astype(jnp.bfloat16)
            if rows < staged.shape[1]:
                rest = staged.shape[1] - rows
                staged[index, rows:] = jnp.zeros((rest, C), jnp.bfloat16)

    def pair_start(buffers, turn):
        staged, landed = buffers[:2]
        other = 1 - frame
        copy = remote(
            staged.at[pl.ds(other * n_row, n_row)], landed,
            first_sem + turn * n_row, (seg, other, row),
        )
        copy.start()
        pending.append((None, copy))
        return copy

    def line_start(buffers, turn, pair):
        staged, landed, added, arrived = buffers
        pair.wait_recv()
        copies = []
        for step in range(n_row - 1, 0, -1):
            target = (row + step) % n_row
            mine = staged[frame * n_row + target].astype(jnp.float32)
            added[target] = (mine + landed[target].astype(jnp.float32)).astype(jnp.bfloat16)
            copy = remote(
                added.at[target], arrived.at[step - 1],
                first_sem + turn * n_row + step, (seg, frame, target),
            )
            copy.start()
            pending.append((None, copy))
            copies.append((step, copy))
        return copies

    def line_finish(buffers, copies, result):
        staged, landed, added, arrived = buffers
        total = staged[frame * n_row + row].astype(jnp.float32) + landed[row].astype(jnp.float32)
        for step, copy in copies:
            copy.wait_recv()
            total = total + arrived[step - 1].astype(jnp.float32)
        result[...] = total[: result.shape[0]]

    def spatial_pass(padded, wide, sem, term):
        halo = row_start(padded, sem)
        widen(padded, wide, BLOCK, CELLS)
        total = term(1)
        halo_wait(halo)
        widen(padded, wide, 0, BLOCK)
        widen(padded, wide, 3 * BLOCK, BLOCK)
        return total + term(0) + term(2)

    def temporal_pass(padded, sem, term):
        halo = frame_start(padded, sem)
        total = term(1)
        halo_wait(halo)
        return total + term(0) + term(2)

    def turn():
        x_turned[...] = jnp.transpose(wide_x[...], (1, 0))
        a_turned[...] = jnp.transpose(pad_a[...], (1, 0))

    def turn_weights():
        for k in range(3):
            tkernel_back[k] = jnp.transpose(tkernel[2 - k], (1, 0))
        for a in range(3):
            for b in range(3):
                tap = kernel[2 - a, pl.ds((2 - b) * C, C), :]
                kernel_back[a, pl.ds(b * C, C), :] = jnp.transpose(tap, (1, 0))

    def temporal_grad():
        for k in range(3):
            temporal_sum[pl.ds(k * C, C), :] = dot_nn(
                a_turned[:, pl.ds(k * BLOCK, CELLS)], pad_u[own, :]
            )
        if fused:
            stage(temporal_sum, reduction[2:6])

    own = pl.ds(BLOCK, CELLS)
    pl.when(seg > 0)(turn_weights)

    @pl.when(seg == 0)
    def _():
        pad_x[own, :] = jnp.zeros((CELLS, C), jnp.bfloat16)
        for r in range(R_DEV):
            for f in range(F_DEV):
                for clip in range(CLIPS):
                    start = BLOCK + ((r * F_DEV + f) * CLIPS + clip) * PAD
                    pad_x[pl.ds(start, WIDTH), :] = latents[clip, f, r]

    @pl.when(seg > 0)
    def _():
        x_copy.wait_recv()

    @pl.when((seg > 0) & (seg < last))
    def _():
        pad_x[own, :] = x_in[...]

    @pl.when(seg == last)
    def _():
        skip_copy.wait_recv()
        joined = x_in[...].astype(jnp.float32) + skip_in[...].astype(jnp.float32)
        pad_x[own, :] = joined.astype(jnp.bfloat16)

    hidden = spatial_pass(
        pad_x, wide_x, 2,
        lambda a: dot_nn(wide_x[pl.ds(a * BLOCK, CELLS), :], kernel[a]),
    )
    normed[...] = hidden.reshape(normed.shape)
    rows = []
    for clip in range(CLIPS):
        part = normed[:, clip] + bias[pl.ds(clip, 1), :].reshape(1, 1, C)
        normed[:, clip] = part
        masked = part * mask[:, clip]
        rows += [column_sum(masked), column_sum(masked * part)]
    stats = exchange_start(0, rows)
    stats = grouped(exchange_wait(stats))
    inverses = []
    for clip in range(CLIPS):
        mean = stats[2 * clip : 2 * clip + 1]
        variance = stats[2 * clip + 1 : 2 * clip + 2] - mean * mean
        inverse = lax.rsqrt(variance + EPSILON)
        inverses.append(inverse)
        part = (normed[:, clip] - mean.reshape(1, 1, C)) * inverse.reshape(1, 1, C)
        normed[:, clip] = part
        scaled = part * gain[...].reshape(1, 1, C)
        grads[:, clip] = mask[:, clip] * (scaled * jax.nn.sigmoid(scaled))
    pad_a[own, :] = swap_order(grads[...].reshape(CELLS, C)).astype(jnp.bfloat16)
    temporal = temporal_pass(
        pad_a, 4, lambda k: dot_nn(pad_a[pl.ds(k * BLOCK, CELLS), :], tkernel[k])
    )

    @pl.when(seg < last)
    def _():
        x_out[...] = (pad_x[own, :].astype(jnp.float32) + swap_order(temporal)).astype(jnp.bfloat16)

    start_if(seg < last, x_copy)
    start_if(seg == 0, skip_copy)
    pl.when(seg < last)(turn)
    pl.when(seg == 0)(turn_weights)

    @pl.when(seg == last)
    def _():
        pad_u[own, :] = jnp.zeros((CELLS, C), jnp.bfloat16)
        for r in range(R_DEV):
            for f in range(F_DEV):
                for clip in range(CLIPS):
                    start = BLOCK + ((f * R_DEV + r) * CLIPS + clip) * PAD
                    kept = mask[r * F_DEV + f, clip][:WIDTH]
                    value = kept * cotangent[clip, f, r].astype(jnp.float32)
                    pad_u[pl.ds(start, WIDTH), :] = value.astype(jnp.bfloat16)

    @pl.when(seg < last)
    def _():
        u_copy.wait_recv()

    @pl.when((seg > 0) & (seg < last))
    def _():
        pad_u[own, :] = swap_order(u_in[...])

    @pl.when(seg == 0)
    def _():
        u_skip_copy.wait_recv()
        joined = u_in[...].astype(jnp.float32) + u_skip[...].astype(jnp.float32)
        pad_u[own, :] = swap_order(joined.astype(jnp.bfloat16))

    act_grad = temporal_pass(
        pad_u, 6, lambda k: dot_nn(pad_u[pl.ds(k * BLOCK, CELLS), :], tkernel_back[k])
    )
    grads[...] = swap_order(act_grad).reshape(grads.shape)
    rows = []
    gain_part = jnp.zeros((1, C), jnp.float32)
    for clip in range(CLIPS):
        part = normed[:, clip]
        scaled = part * gain[...].reshape(1, 1, C)
        gate = jax.nn.sigmoid(scaled)
        scaled_grad = grads[:, clip] * mask[:, clip] * gate * (1.0 + scaled * (1.0 - gate))
        gain_part = gain_part + column_sum(scaled_grad * part)
        normed_grad = scaled_grad * gain[...].reshape(1, 1, C)
        grads[:, clip] = normed_grad
        rows += [column_sum(normed_grad), column_sum(normed_grad * part)]
    moments = exchange_start(1, rows)
    pl.when(seg == 0)(temporal_grad)
    moments = grouped(exchange_wait(moments))
    rows = []
    for clip in range(CLIPS):
        first = moments[2 * clip : 2 * clip + 1].reshape(1, 1, C)
        second = moments[2 * clip + 1 : 2 * clip + 2].reshape(1, 1, C)
        part = inverses[clip].reshape(1, 1, C) * (
            grads[:, clip] - mask[:, clip] * (first + normed[:, clip] * second)
        )
        part = part.astype(jnp.bfloat16).astype(jnp.float32)
        grads[:, clip] = part
        rows.append(column_sum(part))
    pad_h[own, :] = grads[...].reshape(CELLS, C).astype(jnp.bfloat16)
    @pl.when(seg > 0)
    def _():
        pending_before = len(pending)
        back = spatial_pass(
            pad_h, wide_h, 8,
            lambda a: dot_nn(wide_h[pl.ds(a * BLOCK, CELLS), :], kernel_back[a]),
        )
        upstream = swap_order(pad_u[own, :]).astype(jnp.float32)
        u_out[...] = (upstream + back * width_mask[...]).astype(jnp.bfloat16)
        u_copy.start()
        for condition, copy in pending[pending_before:]:
            pl.when(condition)(copy.wait_send)
        del pending[pending_before:]

    @pl.when(seg == last)
    def _():
        u_skip_copy.start()
        turn()

    pl.when(seg > 0)(temporal_grad)
    sums = exchange_start(2, rows + [gain_part])
    if fused:
        temporal_pair = pair_start(reduction[2:6], 0)
    for a in range(3):
        if fused and a == 1:
            temporal_line = line_start(reduction[2:6], 0, temporal_pair)
        spatial_sum[pl.ds(3 * a * C, 3 * C), :] = dot_nn(
            x_turned[:, pl.ds(a * BLOCK, CELLS)], pad_h[own, :]
        )
    if fused:
        stage(spatial_sum, reduction[6:10])
        spatial_line = line_start(reduction[6:10], 1, pair_start(reduction[6:10], 1))
        line_finish(reduction[2:6], temporal_line, temporal_out)
        line_finish(reduction[6:10], spatial_line, spatial_out)
    sums_out[...] = exchange_wait(sums)
    for condition, copy in pending + [(seg > 0, u_copy), (seg == last, u_skip_copy)]:
        if condition is None:
            copy.wait_send()
        else:
            pl.when(condition)(copy.wait_send)


def run_section(sections, n_frame, n_row, *operands):
    peers = n_frame * n_row
    fused = n_frame == 2 and C * 3 % (8 * peers) == 0
    flat = pltpu.VMEM((CELLS, C), jnp.bfloat16)
    padded = pltpu.VMEM((2 * CELLS, C), jnp.bfloat16)
    field = pltpu.VMEM((R_DEV * F_DEV, CLIPS, PAD, C), jnp.float32)
    sems = 12 + 3 * (peers - 1) + 2 * n_row
    vmem = pl.BlockSpec(memory_space=pltpu.VMEM)
    smem = pl.BlockSpec(memory_space=pltpu.SMEM)
    taps = (3, 9)
    share = peers if fused else 1
    reduction = []
    if fused:
        reduction = [pltpu.VMEM((count * C, C), jnp.float32) for count in taps]
        for count in taps:
            rows = -(-count * C // (16 * peers)) * 16
            reduction += [
                pltpu.VMEM((held, rows, C), jnp.bfloat16) for held in (peers, n_row, n_row, n_row - 1)
            ]
    return pl.pallas_call(
        functools.partial(section_kernel, sections, n_frame, n_row),
        out_shape=(
            jax.ShapeDtypeStruct((9 * C // share, C), jnp.float32),
            jax.ShapeDtypeStruct((3 * C // share, C), jnp.float32),
            jax.ShapeDtypeStruct((8, C), jnp.float32),
        ),
        in_specs=[smem] + [vmem] * (len(operands) - 1),
        out_specs=(vmem, vmem, vmem),
        scratch_shapes=[flat] * 6
        + [padded] * 4
        + [pltpu.VMEM((2 * CELLS, 3 * C), jnp.bfloat16)] * 2
        + [
            pltpu.VMEM((3 * C, 2 * CELLS), jnp.bfloat16),
            pltpu.VMEM((C, 2 * CELLS), jnp.bfloat16),
            field,
            field,
            pltpu.VMEM((3, 8, C), jnp.float32),
            pltpu.VMEM((3, peers - 1, 8, C), jnp.float32),
            pltpu.VMEM((R_DEV * F_DEV, CLIPS, PAD, 1), jnp.float32),
            pltpu.VMEM((CELLS, 1), jnp.float32),
            pltpu.VMEM((C, C), jnp.float32),
            pltpu.VMEM((16, C), jnp.float32),
            pltpu.VMEM((3, 3 * C, C), jnp.bfloat16),
            pltpu.VMEM((3, C, C), jnp.bfloat16),
            pltpu.SemaphoreType.DMA((sems,)),
            pltpu.SemaphoreType.DMA((sems,)),
        ]
        + reduction,
        compiler_params=pltpu.CompilerParams(
            collective_id=0, has_side_effects=True, vmem_limit_bytes=56 * 1024 * 1024
        ),
    )(*operands)


def per_device(
    latents,
    cotangent,
    timesteps,
    frame_counts,
    spatial_weight,
    temporal_weight,
    time_weight,
    norm_gain,
):
    sections = lax.axis_size("segment")
    n_frame = lax.axis_size("frame")
    n_row = lax.axis_size("row")
    peers = n_frame * n_row
    me = lax.axis_index("frame") * n_row + lax.axis_index("row")
    time_embed = time_features(jnp.pad(timesteps, (0, 16 - CLIPS)))
    spatial, temporal, sums = run_section(
        sections,
        n_frame,
        n_row,
        frame_counts,
        latents,
        cotangent,
        time_embed,
        spatial_weight[0].reshape(3, 3 * C, C),
        temporal_weight[0],
        time_weight[0],
        norm_gain,
    )
    if spatial.shape[0] == 9 * C:
        parts = [spatial.reshape(peers, -1, C), temporal.reshape(peers, -1, C)]
        parts = jnp.concatenate(parts, axis=1).astype(jnp.bfloat16)
        reduced = lax.psum_scatter(parts, ("frame", "row"), scatter_dimension=0, tiled=True)[0]
        reduced = reduced.astype(jnp.float32)
        spatial, temporal = reduced[: 9 * C // peers], reduced[9 * C // peers :]
    time_rows = TE // peers
    embed = lax.dynamic_slice_in_dim(time_embed, me * time_rows, time_rows, 1).astype(jnp.float32)
    time_out = embed[0][:, None] * sums[0][None, :]
    for clip in range(1, CLIPS):
        time_out = time_out + embed[clip][:, None] * sums[clip][None, :]
    gain_out = lax.dynamic_slice_in_dim(sums[CLIPS], me * (C // peers), C // peers, 0)
    return (spatial[None], temporal[None], time_out[None], gain_out[None])


def solution(mesh):
    return jax.shard_map(
        per_device,
        mesh=mesh,
        in_specs=(
            P(None, "frame", "row", None, None),
            P(None, "frame", "row", None, None),
            P(),
            P(),
            P("segment", None, None, None),
            P("segment", None, None, None),
            P("segment", None, None),
            P("segment", None),
        ),
        out_specs=(
            P("segment", ("frame", "row"), None),
            P("segment", ("frame", "row"), None),
            P("segment", ("frame", "row"), None),
            P("segment", ("frame", "row")),
        ),
        check_vma=False,
    )
```
